512 devices in a mesh: dp: 32 (over y, x_lo, core), owner: 16 (over z, x_hi).
Axes of the slice: x: 4 (x_hi: 2, x_lo: 2; x = x_hi * 2 + x_lo), y: 8, z: 8, core: 2. Of those that a mesh axis runs over, the one named last changes fastest.
Arguments:
- grad_parts: bfloat16 [32, 16, 512, 512], P('dp', 'owner'), may hold values from -0.4375 to 0.4375
- assign: int32 [16], replicated, may hold values from 0 to 15, as said below
- left_basis: bfloat16 [16, 3, 512, 512], P('owner', None, 'dp'), may hold values from -0.25 to 0.25
- right_basis: bfloat16 [16, 3, 512, 512], P('owner', None, 'dp'), may hold values from -0.25 to 0.25
- left_stat: float32 [16, 3, 512, 512], P('owner', None, 'dp'), may hold values from -0.15625 to 0.15625
- right_stat: float32 [16, 3, 512, 512], P('owner', None, 'dp'), may hold values from -0.15625 to 0.15625
- moment: float32 [16, 3, 512, 512], P('owner', None, 'dp'), may hold values from -1.5 to 1.5
- second: float32 [16, 3, 512, 512], P('owner', None, 'dp'), may hold values from 0.001 to 0.01
Outputs:
- update: bfloat16 [16, 512, 512], P('owner', 'dp')
- new_left: float32 [16, 3, 512, 512], P('owner', None, 'dp')
- new_right: float32 [16, 3, 512, 512], P('owner', None, 'dp')
- new_moment: float32 [16, 3, 512, 512], P('owner', None, 'dp')
- new_second: float32 [16, 3, 512, 512], P('owner', None, 'dp')
The draws below stay inside these ranges and needn't reach their ends.
Inputs may be any that keep to these rules, and one draw needn't show every extreme that they name: `assign`: each owner keeps at most 3 blocks and one owner exactly 3; some owners keep none; owners 0 and 15 both keep blocks.
All inputs are finite; a program needn't handle non-finite values.
Results may differ from the reference program's by a relative error of at most 0.024.
Values may be sent and summed in bfloat16 or wider, within the bound.
No kernel may reach another device: no remote copies, remote signals or barrier semaphores. Data moves between devices by JAX's collectives and lax.ppermute only.
A program may use at most 64 MiB of HBM per device.

```python
import math
import jax
import jax.numpy as jnp
from jax import lax

BLOCK = 512
CAP = 3
NBLOCKS = 16
N_DP = 32
N_OWNER = 16


def draw_assign(key, part):
    key = jax.random.fold_in(key, 11)
    coin_key, owner_key, block_key = jax.random.split(key, 3)
    coin = jax.random.randint(coin_key, (), 0, 2).astype(jnp.int32)
    first_two = jnp.where(coin == 0, jnp.array([0, N_OWNER - 1], jnp.int32), jnp.array([N_OWNER - 1, 0], jnp.int32)).astype(jnp.int32)
    middle = jax.random.permutation(owner_key, jnp.arange(1, N_OWNER - 1, dtype=jnp.int32)).astype(jnp.int32)
    owner_order = jnp.concatenate([first_two, middle]).astype(jnp.int32)
    block_order = jax.random.permutation(block_key, NBLOCKS).astype(jnp.int32)
    ranks = jnp.arange(NBLOCKS, dtype=jnp.int32)
    spread = max(N_OWNER // 2, 1)
    owner_rank = jnp.where(ranks < CAP, 0, 1 + (ranks - CAP) % spread).astype(jnp.int32)
    table = jnp.zeros((NBLOCKS,), jnp.int32).at[block_order].set(owner_order[owner_rank])
    return table


def spiked(values, own_key, source, target, blocks, factor):
    def block_of(position):
        return (jnp.arange(values.shape[position]) // (values.shape[position] // blocks)).reshape((-1,) + (1,) * (values.ndim - 1 - position))

    one_side = jax.random.permutation(own_key, blocks)[block_of(target)]
    other_side = (block_of(target) + blocks // 2) % blocks
    return jnp.where((block_of(source) == one_side) | (block_of(source) == other_side), factor * values, values)


def shard_levels(own_key, dims, cuts, smallest, high):
    factor_of, own = 1.0, jax.random.fold_in(own_key, 6)
    for dim, shards_of in cuts:
        steps = jnp.exp(jax.random.uniform(jax.random.fold_in(own, dim), (shards_of,), jnp.float32, smallest / len(cuts), high / len(cuts)))
        factor_of = factor_of * jnp.repeat(steps, dims[dim] // shards_of).reshape([-1 if axis == dim else 1 for axis in range(len(dims))])
    return factor_of


def noise(key, dims, width, bound, cuts=(), kind=jnp.bfloat16):
    result = width * jax.random.normal(key, dims, jnp.float32)
    if cuts:
        result = result * shard_levels(key, dims, cuts, -0.22, 0.18)
    return jnp.clip(result, -bound, bound).astype(kind)


def heavy_noise(rng, extent, scale, most, pieces, heavy, kind=jnp.bfloat16):
    values = scale * jax.random.normal(rng, extent, jnp.float32)
    if pieces:
        values = values * shard_levels(rng, extent, pieces, -0.22, 0.18)
    return jnp.clip(spiked(values, jax.random.fold_in(rng, 3), *heavy), -most, most).astype(kind)


def setup_inputs(seed: int = 0) -> dict:
    key_of = jax.random.split(jax.random.key(seed), 9)
    grad_parts = heavy_noise(key_of[0], (N_DP, NBLOCKS, BLOCK, BLOCK), 0.016, 0.4375, ((0, 32), (1, 16)), (0, 2, 32, 2.75))
    assign = draw_assign(jax.random.fold_in(key_of[8], 71), 0)
    left_basis = noise(key_of[2], (N_OWNER, CAP, BLOCK, BLOCK), BLOCK ** -0.5, 0.25, ((0, 16), (2, 32)))
    right_basis = noise(key_of[3], (N_OWNER, CAP, BLOCK, BLOCK), BLOCK ** -0.5, 0.25, ((0, 16), (2, 32)))
    left_stat = noise(key_of[4], (N_OWNER, CAP, BLOCK, BLOCK), 0.01, 0.15625, ((0, 16), (2, 32)), jnp.float32)
    right_stat = noise(key_of[5], (N_OWNER, CAP, BLOCK, BLOCK), 0.01, 0.15625, ((0, 16), (2, 32)), jnp.float32)
    moment = noise(key_of[6], (N_OWNER, CAP, BLOCK, BLOCK), 0.1, 1.5, ((0, 16), (2, 32)), jnp.float32)
    second = jnp.clip(jnp.exp(math.log(0.01) - 2.30258502 * jax.random.uniform(key_of[7], (N_OWNER, CAP, BLOCK, BLOCK), jnp.float32) ** shard_levels(key_of[7], (N_OWNER, CAP, BLOCK, BLOCK), ((0, 16), (2, 32)), -0.2, 0.2)), 0.001, 0.01)
    return dict(grad_parts=grad_parts, assign=assign, left_basis=left_basis, right_basis=right_basis, left_stat=left_stat, right_stat=right_stat, moment=moment, second=second)


beta_one = 0.9
beta_two = 0.95
step_count = 10.0
adam_eps = 1e-08
bias_one = 1.0 - beta_one ** step_count
bias_two = 1.0 - beta_two ** step_count

def slot_numbers(assign):
    positions = jnp.arange(assign.shape[0], dtype=jnp.int32)
    matching = assign[:, None] == assign[None, :]
    earlier = positions[None, :] < positions[:, None]
    return lax.optimization_barrier(jnp.sum((matching & earlier).astype(jnp.int32), axis=1)).astype(jnp.int32)

def soap_block(grad_block, left_basis, right_basis, left_stat, right_stat, moment, second):
    grad_half = grad_block.astype(jnp.bfloat16)
    left_term = jnp.dot(grad_half, grad_half.T, preferred_element_type=jnp.float32)
    right_term = jnp.dot(grad_half.T, grad_half, preferred_element_type=jnp.float32)
    new_left = beta_two * left_stat + (1.0 - beta_two) * left_term
    new_right = beta_two * right_stat + (1.0 - beta_two) * right_term
    turned = jnp.dot(left_basis.T, grad_half, preferred_element_type=jnp.float32).astype(jnp.bfloat16)
    rotated = jnp.dot(turned, right_basis, preferred_element_type=jnp.float32)
    new_moment = beta_one * moment + (1.0 - beta_one) * rotated
    new_second = beta_two * second + (1.0 - beta_two) * rotated * rotated
    direction = (new_moment / bias_one / (jnp.sqrt(new_second / bias_two) + adam_eps)).astype(jnp.bfloat16)
    back_half = jnp.dot(direction, right_basis.T, preferred_element_type=jnp.float32).astype(jnp.bfloat16)
    slot_update = jnp.dot(left_basis, back_half, preferred_element_type=jnp.float32).astype(jnp.bfloat16)
    return (slot_update, new_left, new_right, new_moment, new_second)

def reference(grad_parts, assign, left_basis, right_basis, left_stat, right_stat, moment, second):
    summed_grad = lax.optimization_barrier(jnp.sum(grad_parts.astype(jnp.float32), axis=0))
    slot_code = (assign * CAP + slot_numbers(assign)).astype(jnp.int32)
    block_ids = jnp.arange(NBLOCKS, dtype=jnp.int32)

    def per_slot(slot_flat):
        matches = slot_code == slot_flat
        source = jnp.sum(jnp.where(matches, block_ids, 0)).astype(jnp.int32)
        present = jnp.any(matches)
        grad_block = jnp.where(present, summed_grad[source], jnp.zeros_like(summed_grad[0]))
        owner_pos = (slot_flat // CAP).astype(jnp.int32)
        slot_pos = (slot_flat % CAP).astype(jnp.int32)
        return soap_block(grad_block, left_basis[owner_pos, slot_pos], right_basis[owner_pos, slot_pos], left_stat[owner_pos, slot_pos], right_stat[owner_pos, slot_pos], moment[owner_pos, slot_pos], second[owner_pos, slot_pos])
    results = lax.map(per_slot, jnp.arange(N_OWNER * CAP, dtype=jnp.int32))
    slot_update, new_left, new_right, new_moment, new_second = results
    update = slot_update[slot_code]
    shape_four = (N_OWNER, CAP, BLOCK, BLOCK)
    return (update, new_left.reshape(shape_four), new_right.reshape(shape_four), new_moment.reshape(shape_four), new_second.reshape(shape_four))
```

```python
import jax
import jax.numpy as jnp
from jax import lax
from jax.sharding import PartitionSpec as P

beta_one = 0.9
beta_two = 0.95
step_count = 10.0
adam_eps = 1e-08
bias_one = 1.0 - beta_one**step_count
bias_two = 1.0 - beta_two**step_count

Y_NUM = 8
XC_NUM = 4


def slot_numbers(assign):
    positions = jnp.arange(assign.shape[0], dtype=jnp.int32)
    matching = assign[:, None] == assign[None, :]
    earlier = positions[None, :] < positions[:, None]
    return jnp.sum((matching & earlier).astype(jnp.int32), axis=1)


def swap_bit(value, bit, size):
    return lax.ppermute(value, "dp", [(i, i ^ bit) for i in range(size)])


def finish_gather(over_y, size):
    index = lax.axis_index("dp")
    x_bit = (index // 2) % 2
    core_bit = index % 2
    other = swap_bit(over_y, 2, size)
    pair = jnp.where(
        x_bit == 0, jnp.stack([over_y, other], 1), jnp.stack([other, over_y], 1)
    )
    other = swap_bit(pair, 1, size)
    quad = jnp.where(core_bit == 0, jnp.stack([pair, other], 2), jnp.stack([other, pair], 2))
    y_num, x_num, core_num, slots, rows, cols = quad.shape
    return quad.transpose(3, 0, 1, 2, 4, 5).reshape(slots, y_num * x_num * core_num * rows, cols)


def y_groups():
    return [[y * XC_NUM + rest for y in range(Y_NUM)] for rest in range(XC_NUM)]


def gather_exchange(rows):
    size = lax.axis_size("dp")
    copies = jnp.broadcast_to(rows[None], (Y_NUM,) + rows.shape)
    over_y = lax.all_to_all(copies, "dp", 0, 0, axis_index_groups=y_groups())
    return finish_gather(over_y, size)


def gather_permutes(rows):
    size = lax.axis_size("dp")
    index = lax.axis_index("dp")
    y_index = index // XC_NUM
    pieces = [rows]
    for step in range(1, Y_NUM):
        pieces.append(
            lax.ppermute(rows, "dp", [(i, (i + step * XC_NUM) % size) for i in range(size)])
        )
    stacked = jnp.stack(pieces, 0)
    order = (y_index - jnp.arange(Y_NUM)) % Y_NUM
    over_y = stacked[order]
    return finish_gather(over_y, size)


def on_device(grad_parts, assign, left_basis, right_basis, left_stat, right_stat, moment, second):
    row_index = lax.axis_index("dp")
    owner_index = lax.axis_index("owner")
    dp_num = lax.axis_size("dp")
    owner_num = lax.axis_size("owner")
    col_num = grad_parts.shape[3]
    row_num = col_num // dp_num
    slot_cap = left_basis.shape[1]
    numbers = slot_numbers(assign)
    left_rows = left_basis[0]
    right_rows = right_basis[0]

    right_full = gather_permutes(right_rows)

    parts = lax.all_to_all(grad_parts.reshape(dp_num, row_num, col_num), "dp", 0, 0)
    left_cut = left_rows.reshape(slot_cap, row_num, dp_num, row_num).transpose(2, 0, 1, 3)
    left_cols = lax.all_to_all(left_cut, "dp", 0, 0)
    left_cols = left_cols.transpose(1, 3, 0, 2).reshape(slot_cap, row_num, col_num)

    grad_half = jnp.sum(parts.astype(jnp.float32), axis=0).astype(jnp.bfloat16)
    blocks = lax.all_to_all(
        jnp.broadcast_to(grad_half[None], (owner_num, row_num, col_num)), "owner", 0, 0
    )
    slot_range = jnp.arange(slot_cap, dtype=jnp.int32)
    pick = ((assign == owner_index)[None, :] & (numbers[None, :] == slot_range[:, None]))
    slot_grad = jnp.einsum(
        "sn,nrc->src",
        pick.astype(jnp.bfloat16),
        blocks,
        preferred_element_type=jnp.float32,
    ).astype(jnp.bfloat16)

    full_grad = gather_exchange(slot_grad)
    own_cols = lax.dynamic_slice_in_dim(full_grad, row_index * row_num, row_num, 2)
    left_term = jnp.einsum(
        "kab,knb->kan", slot_grad, full_grad, preferred_element_type=jnp.float32
    )
    right_term = jnp.einsum(
        "knc,knb->kcb", own_cols, full_grad, preferred_element_type=jnp.float32
    )
    turned = jnp.einsum("kcn,knb->kcb", left_cols, full_grad, preferred_element_type=jnp.float32)
    rotated = jnp.einsum(
        "kab,kbc->kac", turned.astype(jnp.bfloat16), right_full, preferred_element_type=jnp.float32
    )
    new_moment = beta_one * moment[0] + (1.0 - beta_one) * rotated
    new_second = beta_two * second[0] + (1.0 - beta_two) * rotated * rotated
    direction = (new_moment / bias_one / (jnp.sqrt(new_second / bias_two) + adam_eps)).astype(
        jnp.bfloat16
    )
    back_half = jnp.einsum(
        "kac,kbc->kab", direction, right_full, preferred_element_type=jnp.float32
    ).astype(jnp.bfloat16)
    back_full = gather_exchange(back_half)
    slot_update = jnp.einsum(
        "kan,knb->kab", left_rows, back_full, preferred_element_type=jnp.float32
    ).astype(jnp.bfloat16)

    home_pick = (numbers[:, None] == slot_range[None, :]) & (assign == owner_index)[:, None]
    outgoing = jnp.einsum(
        "os,src->orc",
        home_pick.astype(jnp.bfloat16),
        slot_update,
        preferred_element_type=jnp.float32,
    ).astype(jnp.bfloat16)
    incoming = lax.all_to_all(outgoing, "owner", 0, 0)
    update = lax.dynamic_index_in_dim(incoming, assign[owner_index], 0, keepdims=True)

    new_left = beta_two * left_stat[0] + (1.0 - beta_two) * left_term
    new_right = beta_two * right_stat[0] + (1.0 - beta_two) * right_term
    return (update, new_left[None], new_right[None], new_moment[None], new_second[None])


def solution(mesh):
    placed = (
        P("dp", "owner", None, None),
        P(),
        P("owner", None, "dp", None),
        P("owner", None, "dp", None),
        P("owner", None, "dp", None),
        P("owner", None, "dp", None),
        P("owner", None, "dp", None),
        P("owner", None, "dp", None),
    )
    return jax.shard_map(
        on_device,
        mesh=mesh,
        in_specs=placed,
        out_specs=(
            P("owner", "dp", None),
            P("owner", None, "dp", None),
            P("owner", None, "dp", None),
            P("owner", None, "dp", None),
            P("owner", None, "dp", None),
        ),
        check_vma=False,
    )
```

```python
import jax
import jax.numpy as jnp
from jax import lax
from jax.sharding import PartitionSpec as P

beta_one = 0.9
beta_two = 0.95
step_count = 10.0
adam_eps = 1e-08
bias_one = 1.0 - beta_one**step_count
bias_two = 1.0 - beta_two**step_count

LANES = 128
half = jnp.bfloat16


def slot_numbers(assign):
    positions = jnp.arange(assign.shape[0], dtype=jnp.int32)
    matching = assign[:, None] == assign[None, :]
    earlier = positions[None, :] < positions[:, None]
    return jnp.sum((matching & earlier).astype(jnp.int32), axis=1)


def swap_cores(value):
    return lax.ppermute(value, "dp", [(i, i ^ 1) for i in range(lax.axis_size("dp"))])


def exchange(pieces, both_dp):
    chips = lax.axis_size("dp") // 2
    owners = lax.axis_size("owner")
    place = lambda chip, core, owner: (chip * 2 + core) * owners + owner
    groups = [[place(chip, 0, owner) for chip in range(chips)] for owner in range(owners)]
    if both_dp:
        groups += [[place(chip, 1, owner) for chip in range(chips)] for owner in range(owners)]
    else:
        groups += [[place(chip, 1, owner) for owner in range(owners)] for chip in range(chips)]
    return lax.all_to_all(pieces, ("dp", "owner"), 0, 0, axis_index_groups=groups)


def copies(value, count):
    return jnp.broadcast_to(value[None], (count,) + value.shape)


def dot(left, right, contract):
    return lax.dot_general(
        left, right, ((contract[:1], contract[1:]), ((), ())), preferred_element_type=jnp.float32
    )


def on_device(grad_parts, assign, left_basis, right_basis, left_stat, right_stat, moment, second):
    row_index = lax.axis_index("dp")
    owner = lax.axis_index("owner")
    dp_num = lax.axis_size("dp")
    owner_num = lax.axis_size("owner")
    col_num = grad_parts.shape[3]
    row_num = col_num // dp_num
    slot_cap = left_basis.shape[1]
    chunk_num = col_num // LANES
    chips = dp_num // 2
    chip = row_index // 2
    first = row_index % 2 == 0
    chip_rows = 2 * row_num
    kinds = 4

    grads = grad_parts[0, 0]
    slots = jnp.stack(
        [left_basis[0], right_basis[0], moment[0].astype(half), second[0].astype(half)], 1
    )
    slot_rows = slots.reshape(-1, col_num)
    came = swap_cores(
        jnp.where(first, jnp.concatenate([slot_rows, grads[slot_rows.shape[0] :]], 0), grads)
    )
    numbers = slot_numbers(assign)
    chip_grads = jnp.stack(
        [grads.reshape(chips, chip_rows, col_num), came.reshape(chips, chip_rows, col_num)], 1
    ).reshape(chips, 2 * chip_rows, col_num)
    chip_grads = jnp.concatenate([chip_grads, chip_grads], 1)
    chip_slots = jnp.stack([came[: slot_rows.shape[0]].reshape(slots.shape), slots], 2)
    chip_slots = chip_slots.reshape(slot_cap, kinds * chip_rows, col_num)
    number = numbers[:, None, None]
    picked = chip_slots[0][None]
    for slot in range(1, slot_cap):
        picked = jnp.where(number == slot, chip_slots[slot][None], picked)

    parts = exchange(jnp.where(first, chip_grads, picked), False)
    grad_rows = jnp.sum(
        parts[:, : 2 * chip_rows].reshape(2 * chips, chip_rows, col_num).astype(jnp.float32), axis=0
    ).astype(half)
    home = lax.dynamic_index_in_dim(parts, assign[owner], 0, keepdims=False)
    home_came = swap_cores(home)

    left_rows, right_rows = home.reshape(kinds, chip_rows, col_num)[:2]
    left_chunks = left_rows.reshape(chip_rows, chunk_num, LANES).transpose(1, 0, 2)
    left_chunks = jnp.broadcast_to(
        left_chunks[:, None], (chunk_num, chips // chunk_num, chip_rows, LANES)
    ).reshape(chips, chip_rows, LANES)
    rows = copies(jnp.where(first, grad_rows, right_rows), chips)
    mine = exchange(jnp.concatenate([rows, left_chunks], 2), True)
    mine = mine.reshape(col_num, col_num + LANES)
    other = swap_cores(mine)
    grad_full = jnp.where(first, mine[:, :col_num], other[:, :col_num])
    right_full = jnp.where(first, other[:, :col_num], mine[:, :col_num])
    left_cols = jnp.where(first, other[:, col_num:], mine[:, col_num:])
    home = jnp.where(first, home_came, home).reshape(kinds, chip_rows, col_num)

    chunk = chip // (chips // chunk_num)
    in_chunk = (chip % (chips // chunk_num)) * chip_rows
    own_rows = lambda value: lax.dynamic_slice_in_dim(value, in_chunk, chip_rows, 0)
    turned = own_rows(dot(left_cols, grad_full, (0, 0)).astype(half))
    rotated = dot(turned, right_full, (1, 0))
    home_moment = beta_one * home[2].astype(jnp.float32) + (1.0 - beta_one) * rotated
    home_second = beta_two * home[3].astype(jnp.float32) + (1.0 - beta_two) * rotated * rotated
    direction = (home_moment / bias_one / (jnp.sqrt(home_second / bias_two) + adam_eps)).astype(half)
    back_rows = dot(direction, right_full, (1, 1)).astype(half)
    grad_cols = lax.dynamic_slice_in_dim(grad_full, chunk * LANES, LANES, 1)
    chip_grad_rows = lax.dynamic_slice_in_dim(grad_full, chip * chip_rows, chip_rows, 0)
    left_term = dot(chip_grad_rows, grad_full, (1, 1)).astype(half)
    right_term = own_rows(dot(grad_cols, grad_full, (0, 0)).astype(half))

    results = jnp.concatenate(
        [jnp.where(first, back_rows, left_term), right_term, rotated.astype(half)], 0
    )
    gathered = exchange(copies(results, chips), False)
    back_full = gathered[:, :chip_rows].reshape(col_num, col_num)
    chip_update = dot(home[0], back_full, (1, 0)).astype(half)
    held = (assign == owner)[None, :] & (
        numbers[None, :] == jnp.arange(slot_cap, dtype=jnp.int32)[:, None]
    )
    chip_results = jnp.sum(
        jnp.where(held[:, :, None, None], gathered[None].astype(jnp.float32), 0.0), axis=1
    ).astype(half)
    chip_results = chip_results.reshape(slot_cap, 3, 2, row_num, col_num)
    for_first = chip_results[:, :, 0].reshape(-1, col_num)
    for_second = jnp.concatenate([chip_update[row_num:], for_first[row_num:]], 0)
    came = swap_cores(jnp.where(first, for_second, for_first))
    update = jnp.where(first, chip_update[:row_num], came[:row_num])
    terms = jnp.where(
        first, came.reshape(slot_cap, 3, row_num, col_num), chip_results[:, :, 1]
    ).astype(jnp.float32)

    new_left = beta_two * left_stat[0] + (1.0 - beta_two) * terms[:, 0]
    new_right = beta_two * right_stat[0] + (1.0 - beta_two) * terms[:, 1]
    new_moment = beta_one * moment[0] + (1.0 - beta_one) * terms[:, 2]
    new_second = beta_two * second[0] + (1.0 - beta_two) * terms[:, 2] * terms[:, 2]
    return (update[None], new_left[None], new_right[None], new_moment[None], new_second[None])


def solution(mesh):
    placed = (
        P("dp", "owner", None, None),
        P(),
        P("owner", None, "dp", None),
        P("owner", None, "dp", None),
        P("owner", None, "dp", None),
        P("owner", None, "dp", None),
        P("owner", None, "dp", None),
        P("owner", None, "dp", None),
    )
    return jax.shard_map(
        on_device,
        mesh=mesh,
        in_specs=placed,
        out_specs=(
            P("owner", "dp", None),
            P("owner", None, "dp", None),
            P("owner", None, "dp", None),
            P("owner", None, "dp", None),
            P("owner", None, "dp", None),
        ),
        check_vma=False,
    )
```

```python
import jax
import jax.numpy as jnp
from jax import lax
from jax.experimental import pallas as pl
from jax.experimental.pallas import tpu as pltpu
from jax.sharding import PartitionSpec as P

beta_one = 0.9
beta_two = 0.95
step_count = 10.0
adam_eps = 1e-08
bias_one = 1.0 - beta_one**step_count
bias_two = 1.0 - beta_two**step_count

LANES = 128
half = jnp.bfloat16


def slot_numbers(assign):
    positions = jnp.arange(assign.shape[0], dtype=jnp.int32)
    matching = assign[:, None] == assign[None, :]
    earlier = positions[None, :] < positions[:, None]
    return jnp.sum((matching & earlier).astype(jnp.int32), axis=1)


def swap_cores(value):
    return lax.ppermute(value, "dp", [(i, i ^ 1) for i in range(lax.axis_size("dp"))])


def place(chip, core, owner):
    return (chip * 2 + core) * lax.axis_size("owner") + owner


def exchange_dp(pieces):
    chips = lax.axis_size("dp") // 2
    groups = [[chip * 2 + core for chip in range(chips)] for core in range(2)]
    return lax.all_to_all(pieces, "dp", 0, 0, axis_index_groups=groups)


def exchange(pieces):
    chips = lax.axis_size("dp") // 2
    owners = lax.axis_size("owner")
    groups = [[place(chip, 0, owner) for chip in range(chips)] for owner in range(owners)]
    groups += [[place(chip, 1, owner) for owner in range(owners)] for chip in range(chips)]
    return lax.all_to_all(pieces, ("dp", "owner"), 0, 0, axis_index_groups=groups)


def exchange_lines(pieces):
    chips = lax.axis_size("dp") // 2
    owners = lax.axis_size("owner")
    groups = [
        [place(2 * y + x, 0, owner) for y in range(chips // 2)]
        for owner in range(owners)
        for x in range(2)
    ]
    groups += [
        [place(chip, 1, 2 * z + x) for z in range(owners // 2)]
        for chip in range(chips)
        for x in range(2)
    ]
    return lax.all_to_all(pieces, ("dp", "owner"), 0, 0, axis_index_groups=groups)


def swap_x(value):
    chips = lax.axis_size("dp") // 2
    owners = lax.axis_size("owner")
    pairs = []
    for chip in range(chips):
        for owner in range(owners):
            pairs.append((place(chip, 0, owner), place(chip ^ 1, 0, owner)))
            pairs.append((place(chip, 1, owner), place(chip, 1, owner ^ 1)))
    return lax.ppermute(value, ("dp", "owner"), pairs)


def first_payload_kernel(core, grads, left, right, moment, second, slots, payload):
    for slot in range(left.shape[0]):
        slots[slot, 0] = left[slot]
        slots[slot, 1] = right[slot]
        slots[slot, 2] = moment[slot].astype(half)
        slots[slot, 3] = second[slot].astype(half)

    @pl.when(core[0] == 0)
    def _():
        rows = left.shape[1]
        for slot in range(left.shape[0]):
            for kind in range(4):
                payload[pl.ds((slot * 4 + kind) * rows, rows)] = slots[slot, kind]

    @pl.when(core[0] != 0)
    def _():
        payload[...] = grads[...]


def first_payload(core, grads, left, right, moment, second):
    slot_cap, row_num, col_num = left.shape
    vmem = pl.BlockSpec(memory_space=pltpu.VMEM)
    return pl.pallas_call(
        first_payload_kernel,
        out_shape=(
            jax.ShapeDtypeStruct((slot_cap, 4, row_num, col_num), half),
            jax.ShapeDtypeStruct(grads.shape, half),
        ),
        in_specs=[pl.BlockSpec(memory_space=pltpu.SMEM)] + [vmem] * 5,
        out_specs=(vmem, vmem),
        compiler_params=pltpu.CompilerParams(vmem_limit_bytes=16 * 1024 * 1024),
        name="first_payload",
    )(core, grads, left, right, moment, second)


def copies(value, count):
    return jnp.broadcast_to(value[None], (count,) + value.shape)


def dot(left, right, contract):
    return lax.dot_general(
        left, right, ((contract[:1], contract[1:]), ((), ())), preferred_element_type=jnp.float32
    )


def on_device(grad_parts, assign, left_basis, right_basis, left_stat, right_stat, moment, second):
    row_index = lax.axis_index("dp")
    owner = lax.axis_index("owner")
    dp_num = lax.axis_size("dp")
    owner_num = lax.axis_size("owner")
    col_num = grad_parts.shape[3]
    row_num = col_num // dp_num
    slot_cap = left_basis.shape[1]
    chunk_num = col_num // LANES
    chips = dp_num // 2
    chip = row_index // 2
    first = row_index % 2 == 0
    chip_rows = 2 * row_num
    kinds = 4

    grads = grad_parts[0, 0]
    slots, payload = first_payload(
        (row_index % 2).reshape(1), grads, left_basis[0], right_basis[0], moment[0], second[0]
    )
    came = swap_cores(payload)
    numbers = slot_numbers(assign)

    y_num = chips // 2
    z_num = owner_num // 2
    pair = (grads.astype(jnp.float32) + came.astype(jnp.float32)).astype(half)
    pair = pair.reshape(y_num, 2, chip_rows, col_num)
    even = chip % 2 == 0
    kept = jnp.where(even, pair[:, 0], pair[:, 1])
    sent = jnp.where(even, pair[:, 1], pair[:, 0]).reshape(-1, col_num)
    slot_rows = slot_cap * kinds * row_num
    chip_slots = jnp.stack([came[:slot_rows].reshape(slots.shape), slots], 2)
    chip_slots = chip_slots.reshape(slot_cap * kinds * chip_rows, col_num)
    sent_num = sent.shape[0]
    beside = swap_x(
        jnp.concatenate(
            [jnp.where(first, sent, chip_slots[:sent_num]), chip_slots[sent_num:]], 0
        )
    )
    sums = kept.astype(jnp.float32) + beside[:sent_num].reshape(kept.shape).astype(jnp.float32)
    sums = sums.astype(half)

    owner_x = owner % 2
    from_owner = lax.dynamic_index_in_dim(assign.reshape(z_num, 2), owner_x, 1, keepdims=False)
    number = lax.dynamic_index_in_dim(numbers.reshape(z_num, 2), owner_x, 1, keepdims=False)
    code = (number + slot_cap * (from_owner % 2 != owner_x))[:, None, None]
    chip_slots = chip_slots.reshape(slot_cap, kinds * chip_rows, col_num)
    beside = beside.reshape(chip_slots.shape)
    picked = chip_slots[0][None]
    for slot in range(1, slot_cap):
        picked = jnp.where(code == slot, chip_slots[slot][None], picked)
    for slot in range(slot_cap):
        picked = jnp.where(code == slot_cap + slot, beside[slot][None], picked)

    parts = exchange_lines(
        jnp.concatenate(
            [jnp.where(first, sums, picked[:, :chip_rows]), picked[:, chip_rows:]], 1
        )
    )
    grad_rows = jnp.sum(parts[:, :chip_rows].astype(jnp.float32), axis=0).astype(half)
    home = lax.dynamic_index_in_dim(parts, assign[owner] // 2, 0, keepdims=False)

    left_rows, right_rows = home.reshape(kinds, chip_rows, col_num)[:2]
    left_chunks = left_rows.reshape(chip_rows, chunk_num, LANES).transpose(1, 0, 2)
    left_chunks = jnp.broadcast_to(
        left_chunks[:, None], (chunk_num, chips // chunk_num, chip_rows, LANES)
    ).reshape(chips, chip_rows, LANES)
    rows = copies(jnp.where(first, grad_rows, right_rows), chips)
    mine = exchange_dp(jnp.concatenate([rows, left_chunks], 2))
    mine = mine.reshape(col_num, col_num + LANES)
    wide_home = jnp.concatenate([home, home[:, :LANES]], 1)
    other = swap_cores(jnp.concatenate([mine, wide_home], 0))
    home = jnp.where(first, other[col_num:, :col_num], home).reshape(kinds, chip_rows, col_num)
    other = other[:col_num]
    grad_full = jnp.where(first, mine[:, :col_num], other[:, :col_num])
    right_full = jnp.where(first, other[:, :col_num], mine[:, :col_num])
    left_cols = jnp.where(first, other[:, col_num:], mine[:, col_num:])

    chunk = chip // (chips // chunk_num)
    in_chunk = (chip % (chips // chunk_num)) * chip_rows
    own_rows = lambda value: lax.dynamic_slice_in_dim(value, in_chunk, chip_rows, 0)
    turned = own_rows(dot(left_cols, grad_full, (0, 0)).astype(half))
    rotated = dot(turned, right_full, (1, 0))
    home_moment = beta_one * home[2].astype(jnp.float32) + (1.0 - beta_one) * rotated
    home_second = beta_two * home[3].astype(jnp.float32) + (1.0 - beta_two) * rotated * rotated
    direction = (home_moment / bias_one / (jnp.sqrt(home_second / bias_two) + adam_eps)).astype(half)
    back_rows = dot(direction, right_full, (1, 1)).astype(half)
    grad_cols = lax.dynamic_slice_in_dim(grad_full, chunk * LANES, LANES, 1)
    chip_grad_rows = lax.dynamic_slice_in_dim(grad_full, chip * chip_rows, chip_rows, 0)
    left_term = dot(chip_grad_rows, grad_full, (1, 1)).astype(half)
    right_term = own_rows(dot(grad_cols, grad_full, (0, 0)).astype(half))

    results = jnp.concatenate(
        [jnp.where(first, back_rows, left_term), right_term, rotated.astype(half)], 0
    )
    gathered = exchange(copies(results, chips))
    back_full = gathered[:, :chip_rows].reshape(col_num, col_num)
    chip_update = dot(home[0], back_full, (1, 0)).astype(half)
    held = (assign == owner)[None, :] & (
        numbers[None, :] == jnp.arange(slot_cap, dtype=jnp.int32)[:, None]
    )
    chip_results = jnp.sum(
        jnp.where(held[:, :, None, None], gathered[None].astype(jnp.float32), 0.0), axis=1
    ).astype(half)
    chip_results = chip_results.reshape(slot_cap, 3, 2, row_num, col_num)
    for_first = chip_results[:, :, 0].reshape(-1, col_num)
    for_second = jnp.concatenate([chip_update[row_num:], for_first[row_num:]], 0)
    came = swap_cores(jnp.where(first, for_second, for_first))
    update = jnp.where(first, chip_update[:row_num], came[:row_num])
    terms = jnp.where(
        first, came.reshape(slot_cap, 3, row_num, col_num), chip_results[:, :, 1]
    ).astype(jnp.float32)

    new_left = beta_two * left_stat[0] + (1.0 - beta_two) * terms[:, 0]
    new_right = beta_two * right_stat[0] + (1.0 - beta_two) * terms[:, 1]
    new_moment = beta_one * moment[0] + (1.0 - beta_one) * terms[:, 2]
    new_second = beta_two * second[0] + (1.0 - beta_two) * terms[:, 2] * terms[:, 2]
    return (update[None], new_left[None], new_right[None], new_moment[None], new_second[None])


def solution(mesh):
    placed = (
        P("dp", "owner", None, None),
        P(),
        P("owner", None, "dp", None),
        P("owner", None, "dp", None),
        P("owner", None, "dp", None),
        P("owner", None, "dp", None),
        P("owner", None, "dp", None),
        P("owner", None, "dp", None),
    )
    return jax.shard_map(
        on_device,
        mesh=mesh,
        in_specs=placed,
        out_specs=(
            P("owner", "dp", None),
            P("owner", None, "dp", None),
            P("owner", None, "dp", None),
            P("owner", None, "dp", None),
            P("owner", None, "dp", None),
        ),
        check_vma=False,
    )
```

```python
import jax
import jax.numpy as jnp
from jax import lax
from jax.experimental import pallas as pl
from jax.experimental.pallas import tpu as pltpu
from jax.sharding import PartitionSpec as P

beta_one = 0.9
beta_two = 0.95
step_count = 10.0
adam_eps = 1e-08
bias_one = 1.0 - beta_one**step_count
bias_two = 1.0 - beta_two**step_count

LANES = 128
half = jnp.bfloat16


def slot_numbers(assign):
    positions = jnp.arange(assign.shape[0], dtype=jnp.int32)
    matching = assign[:, None] == assign[None, :]
    earlier = positions[None, :] < positions[:, None]
    return jnp.sum((matching & earlier).astype(jnp.int32), axis=1)


def swap_cores(value):
    return lax.ppermute(value, "dp", [(i, i ^ 1) for i in range(lax.axis_size("dp"))])


def place(chip, core, owner):
    return (chip * 2 + core) * lax.axis_size("owner") + owner


def exchange_dp(pieces):
    chips = lax.axis_size("dp") // 2
    groups = [[chip * 2 + core for chip in range(chips)] for core in range(2)]
    return lax.all_to_all(pieces, "dp", 0, 0, axis_index_groups=groups)


def exchange(pieces):
    chips = lax.axis_size("dp") // 2
    owners = lax.axis_size("owner")
    groups = [[place(chip, 0, owner) for chip in range(chips)] for owner in range(owners)]
    groups += [[place(chip, 1, owner) for owner in range(owners)] for chip in range(chips)]
    return lax.all_to_all(pieces, ("dp", "owner"), 0, 0, axis_index_groups=groups)


def exchange_lines(pieces, y_core):
    chips = lax.axis_size("dp") // 2
    owners = lax.axis_size("owner")
    groups = [
        [place(2 * y + x, y_core, owner) for y in range(chips // 2)]
        for owner in range(owners)
        for x in range(2)
    ]
    groups += [
        [place(chip, 1 - y_core, 2 * z + x) for z in range(owners // 2)]
        for chip in range(chips)
        for x in range(2)
    ]
    return lax.all_to_all(pieces, ("dp", "owner"), 0, 0, axis_index_groups=groups)


def swap_x(value):
    chips = lax.axis_size("dp") // 2
    owners = lax.axis_size("owner")
    pairs = []
    for chip in range(chips):
        for owner in range(owners):
            pairs.append((place(chip, 0, owner), place(chip ^ 1, 0, owner)))
            pairs.append((place(chip, 1, owner), place(chip, 1, owner ^ 1)))
    return lax.ppermute(value, ("dp", "owner"), pairs)


def first_payload_kernel(core, grads, left, right, payload, sems):
    slot_cap, row_num = left.shape[1:3]

    @pl.when(core[0] == 0)
    def _():
        moves = []
        for slot in range(slot_cap):
            for kind, basis in enumerate((left, right)):
                place_of = slot * 2 + kind
                moves.append(
                    pltpu.make_async_copy(
                        basis.at[0, slot],
                        payload.at[pl.ds(place_of * row_num, row_num)],
                        sems.at[place_of],
                    )
                )
        for move in moves:
            move.start()
        for move in moves:
            move.wait()

    @pl.when(core[0] != 0)
    def _():
        move = pltpu.make_async_copy(grads.at[0, 0], payload, sems.at[0])
        move.start()
        move.wait()


def first_payload(core, grads, left, right):
    anywhere = pl.BlockSpec(memory_space=pl.ANY)
    return pl.pallas_call(
        first_payload_kernel,
        out_shape=jax.ShapeDtypeStruct(grads.shape[2:], half),
        in_specs=[pl.BlockSpec(memory_space=pltpu.SMEM)] + [anywhere] * 3,
        out_specs=anywhere,
        scratch_shapes=[pltpu.SemaphoreType.DMA((2 * left.shape[1],))],
        compiler_params=pltpu.CompilerParams(vmem_limit_bytes=60 * 1024 * 1024),
        name="first_payload",
    )(core, grads, left, right)


def state_pieces_kernel(assign, moment, second, pieces, wide, narrow, sems):
    moves = [
        pltpu.make_async_copy(source.at[0], wide.at[kind], sems.at[kind])
        for kind, source in enumerate((moment, second))
    ]
    for move in moves:
        move.start()
    for move in moves:
        move.wait()
    slot_cap = moment.shape[1]
    for slot in range(slot_cap):
        for kind in range(2):
            narrow[slot, kind] = wide[kind, slot].astype(half)
    for block in range(assign.shape[0]):
        number = jnp.int32(0)
        for earlier in range(block):
            number += (assign[earlier] == assign[block]).astype(jnp.int32)
        pieces[block] = narrow[jnp.minimum(number, slot_cap - 1)]


def state_pieces(assign, moment, second):
    slot_cap, row_num, col_num = moment.shape[1:]
    anywhere = pl.BlockSpec(memory_space=pl.ANY)
    return pl.pallas_call(
        state_pieces_kernel,
        out_shape=jax.ShapeDtypeStruct((assign.shape[0], 2, row_num, col_num), half),
        in_specs=[pl.BlockSpec(memory_space=pltpu.SMEM), anywhere, anywhere],
        out_specs=pl.BlockSpec(memory_space=pltpu.VMEM),
        scratch_shapes=[
            pltpu.VMEM((2, slot_cap, row_num, col_num), jnp.float32),
            pltpu.VMEM((slot_cap, 2, row_num, col_num), half),
            pltpu.SemaphoreType.DMA((2,)),
        ],
        name="state_pieces",
    )(assign, moment, second)


def copies(value, count):
    return jnp.broadcast_to(value[None], (count,) + value.shape)


def dot(left, right, contract):
    return lax.dot_general(
        left, right, ((contract[:1], contract[1:]), ((), ())), preferred_element_type=jnp.float32
    )


def on_device(grad_parts, assign, left_basis, right_basis, left_stat, right_stat, moment, second):
    row_index = lax.axis_index("dp")
    owner = lax.axis_index("owner")
    dp_num = lax.axis_size("dp")
    owner_num = lax.axis_size("owner")
    col_num = grad_parts.shape[3]
    row_num = col_num // dp_num
    slot_cap = left_basis.shape[1]
    chunk_num = col_num // LANES
    chips = dp_num // 2
    chip = row_index // 2
    first = row_index % 2 == 0
    chip_rows = 2 * row_num
    y_num = chips // 2
    z_num = owner_num // 2
    kinds = 2

    came = swap_cores(
        first_payload((row_index % 2).reshape(1), grad_parts, left_basis, right_basis)
    )

    numbers = slot_numbers(assign)
    states = lax.all_to_all(state_pieces(assign, moment, second), "owner", 0, 0)
    states = lax.dynamic_index_in_dim(states, assign[owner], 0, keepdims=False)

    pair = (grad_parts[0, 0].astype(jnp.float32) + came.astype(jnp.float32)).astype(half)
    pair = pair.reshape(y_num, 2, chip_rows, col_num)
    even = chip % 2 == 0
    kept = jnp.where(even, pair[:, 0], pair[:, 1])
    sent = jnp.where(even, pair[:, 1], pair[:, 0]).reshape(-1, col_num)
    slots = jnp.stack([left_basis[0], right_basis[0]], 1)
    slot_rows = slot_cap * kinds * row_num
    chip_slots = jnp.stack([came[:slot_rows].reshape(slots.shape), slots], 2)
    chip_slots = chip_slots.reshape(slot_cap * kinds * chip_rows, col_num)
    slot_rows = chip_slots.shape[0]
    beside = swap_x(
        jnp.concatenate([jnp.where(first, sent[:slot_rows], chip_slots), sent[slot_rows:]], 0)
    )
    sums = kept.astype(jnp.float32) + beside.reshape(kept.shape).astype(jnp.float32)
    sums = sums.astype(half)

    owner_x = owner % 2
    from_owner = lax.dynamic_index_in_dim(assign.reshape(z_num, 2), owner_x, 1, keepdims=False)
    number = lax.dynamic_index_in_dim(numbers.reshape(z_num, 2), owner_x, 1, keepdims=False)
    code = (number + slot_cap * (from_owner % 2 != owner_x))[:, None, None]
    chip_slots = chip_slots.reshape(slot_cap, kinds * chip_rows, col_num)
    beside = beside[:slot_rows].reshape(chip_slots.shape)
    picked = chip_slots[0][None]
    for slot in range(1, slot_cap):
        picked = jnp.where(code == slot, chip_slots[slot][None], picked)
    for slot in range(slot_cap):
        picked = jnp.where(code == slot_cap + slot, beside[slot][None], picked)

    parts = exchange_lines(
        jnp.concatenate(
            [jnp.where(first, sums, picked[:, :chip_rows]), picked[:, chip_rows:]], 1
        ),
        0,
    )
    grad_rows = jnp.sum(parts[:, :chip_rows].astype(jnp.float32), axis=0).astype(half)
    home = lax.dynamic_index_in_dim(parts, assign[owner] // 2, 0, keepdims=False)

    left_rows, right_rows = home.reshape(kinds, chip_rows, col_num)
    left_chunks = left_rows.reshape(chip_rows, chunk_num, LANES).transpose(1, 0, 2)
    left_chunks = jnp.broadcast_to(
        left_chunks[:, None], (chunk_num, chips // chunk_num, chip_rows, LANES)
    ).reshape(chips, chip_rows, LANES)
    rows = copies(jnp.where(first, grad_rows, right_rows), chips)
    mine = exchange_dp(jnp.concatenate([rows, left_chunks], 2))
    mine = mine.reshape(col_num, col_num + LANES)

    chunk = chip // (chips // chunk_num)
    in_chunk = (chip % (chips // chunk_num)) * chip_rows
    own_rows = lambda value: lax.dynamic_slice_in_dim(value, in_chunk, chip_rows, 0)
    core_full = mine[:, :col_num]
    grad_cols = lax.dynamic_slice_in_dim(core_full, chunk * LANES, LANES, 1)
    left_term = dot(grad_rows, core_full, (1, 1)).astype(half)
    right_term = own_rows(dot(grad_cols, core_full, (0, 0)).astype(half))
    grams = exchange_lines(copies(jnp.concatenate([left_term, right_term], 0), z_num), 1)

    extra = jnp.concatenate([left_rows, states.reshape(-1, col_num)], 0)
    extra = jnp.concatenate([extra, extra[:, :LANES]], 1)
    other = swap_cores(jnp.concatenate([mine, extra], 0))
    left_rows = other[col_num : col_num + chip_rows, :col_num]
    other_states = other[col_num + chip_rows :, :col_num].reshape(states.shape)
    states = jnp.concatenate([states, other_states], 1).astype(jnp.float32)
    other = other[:col_num]
    grad_full = jnp.where(first, core_full, other[:, :col_num])
    right_full = jnp.where(first, other[:, :col_num], core_full)
    left_cols = jnp.where(first, other[:, col_num:], mine[:, col_num:])

    turned = own_rows(dot(left_cols, grad_full, (0, 0)).astype(half))
    rotated = dot(turned, right_full, (1, 0))
    home_moment = beta_one * states[0] + (1.0 - beta_one) * rotated
    home_second = beta_two * states[1] + (1.0 - beta_two) * rotated * rotated
    direction = (home_moment / bias_one / (jnp.sqrt(home_second / bias_two) + adam_eps)).astype(half)
    back_rows = dot(direction, right_full, (1, 1)).astype(half)

    results = copies(jnp.where(first, back_rows, rotated.astype(half)), chips)
    results, grams = lax.optimization_barrier((results, grams))
    gathered = exchange(results)
    held = lambda blocks, counts, target: (blocks == target)[None, :] & (
        counts[None, :] == jnp.arange(slot_cap, dtype=jnp.int32)[:, None]
    )

    def taken(mask, values):
        values = jnp.where(mask[:, :, None, None], values[None].astype(jnp.float32), 0.0)
        return jnp.sum(values, axis=1).astype(half)

    own_grams = taken(held(from_owner, number, owner), grams)
    beside_grams = taken(held(from_owner, number, owner ^ 1), grams)
    owners_beside = [(i, i ^ 1) for i in range(owner_num)]
    own_grams = own_grams + lax.ppermute(beside_grams, "owner", owners_beside)
    own_grams = own_grams.reshape(slot_cap * 2, 2, row_num, col_num)

    back_full = gathered.reshape(col_num, col_num)
    chip_update = dot(left_rows, back_full, (1, 0)).astype(half)
    turns = taken(held(assign, numbers, owner), gathered).reshape(slot_cap, 2, row_num, col_num)
    for_second = jnp.concatenate(
        [chip_update[row_num:], own_grams[:, 1].reshape(-1, col_num)], 0
    )
    turn_rows = slot_cap * row_num
    for_first = jnp.where(first, for_second[:turn_rows], turns[:, 0].reshape(-1, col_num))
    came = swap_cores(jnp.concatenate([for_first, for_second[turn_rows:]], 0))
    update = jnp.where(first, chip_update[:row_num], came[:row_num])
    grams = jnp.where(first, own_grams[:, 0], came[row_num:].reshape(own_grams[:, 0].shape))
    grams = grams.reshape(slot_cap, 2, row_num, col_num).astype(jnp.float32)
    turns = jnp.where(first, came[:turn_rows].reshape(turns[:, 0].shape), turns[:, 1])
    turns = turns.astype(jnp.float32)

    new_left = beta_two * left_stat[0] + (1.0 - beta_two) * grams[:, 0]
    new_right = beta_two * right_stat[0] + (1.0 - beta_two) * grams[:, 1]
    new_moment = beta_one * moment[0] + (1.0 - beta_one) * turns
    new_second = beta_two * second[0] + (1.0 - beta_two) * turns * turns
    return (update[None], new_left[None], new_right[None], new_moment[None], new_second[None])


def solution(mesh):
    placed = (
        P("dp", "owner", None, None),
        P(),
        P("owner", None, "dp", None),
        P("owner", None, "dp", None),
        P("owner", None, "dp", None),
        P("owner", None, "dp", None),
        P("owner", None, "dp", None),
        P("owner", None, "dp", None),
    )
    return jax.shard_map(
        on_device,
        mesh=mesh,
        in_specs=placed,
        out_specs=(
            P("owner", "dp", None),
            P("owner", None, "dp", None),
            P("owner", None, "dp", None),
            P("owner", None, "dp", None),
            P("owner", None, "dp", None),
        ),
        check_vma=False,
    )
```

```python
import jax
import jax.numpy as jnp
from jax import lax
from jax.experimental import pallas as pl
from jax.experimental.pallas import tpu as pltpu
from jax.sharding import PartitionSpec as P

beta_one = 0.9
beta_two = 0.95
step_count = 10.0
adam_eps = 1e-08
bias_one = 1.0 - beta_one**step_count
bias_two = 1.0 - beta_two**step_count

LANES = 128
half = jnp.bfloat16


def slot_numbers(assign):
    positions = jnp.arange(assign.shape[0], dtype=jnp.int32)
    matching = assign[:, None] == assign[None, :]
    earlier = positions[None, :] < positions[:, None]
    return jnp.sum((matching & earlier).astype(jnp.int32), axis=1)


def swap_cores(value):
    return lax.ppermute(value, "dp", [(i, i ^ 1) for i in range(lax.axis_size("dp"))])


def place(chip, core, owner):
    return (chip * 2 + core) * lax.axis_size("owner") + owner


def exchange_dp(pieces):
    chips = lax.axis_size("dp") // 2
    groups = [[chip * 2 + core for chip in range(chips)] for core in range(2)]
    return lax.all_to_all(pieces, "dp", 0, 0, axis_index_groups=groups)


def exchange(pieces):
    chips = lax.axis_size("dp") // 2
    owners = lax.axis_size("owner")
    groups = [[place(chip, 0, owner) for chip in range(chips)] for owner in range(owners)]
    groups += [[place(chip, 1, owner) for owner in range(owners)] for chip in range(chips)]
    return lax.all_to_all(pieces, ("dp", "owner"), 0, 0, axis_index_groups=groups)


def shift_z(value, step):
    owners = lax.axis_size("owner")
    return lax.ppermute(
        value, "owner", [(i, (i + 2 * step) % owners) for i in range(owners)]
    )


def swap_owners(value):
    return lax.ppermute(value, "owner", [(i, i ^ 1) for i in range(lax.axis_size("owner"))])


def z_order(value, z):
    return lax.dynamic_slice_in_dim(jnp.concatenate([value, value], 0), z, value.shape[0], 0)


def first_payload_kernel(core, grads, left, right, payload, sems):
    slot_cap, row_num = left.shape[1:3]

    @pl.when(core[0] == 0)
    def _():
        moves = []
        for slot in range(slot_cap):
            for kind, basis in enumerate((left, right)):
                place_of = slot * 2 + kind
                moves.append(
                    pltpu.make_async_copy(
                        basis.at[0, slot],
                        payload.at[pl.ds(place_of * row_num, row_num)],
                        sems.at[place_of],
                    )
                )
        for move in moves:
            move.start()
        for move in moves:
            move.wait()

    @pl.when(core[0] != 0)
    def _():
        move = pltpu.make_async_copy(grads.at[0, 0], payload, sems.at[0])
        move.start()
        move.wait()


def first_payload(core, grads, left, right):
    anywhere = pl.BlockSpec(memory_space=pl.ANY)
    return pl.pallas_call(
        first_payload_kernel,
        out_shape=jax.ShapeDtypeStruct(grads.shape[2:], half),
        in_specs=[pl.BlockSpec(memory_space=pltpu.SMEM)] + [anywhere] * 3,
        out_specs=pl.BlockSpec(memory_space=pltpu.VMEM),
        scratch_shapes=[pltpu.SemaphoreType.DMA((2 * left.shape[1],))],
        compiler_params=pltpu.CompilerParams(vmem_limit_bytes=60 * 1024 * 1024),
        name="first_payload",
    )(core, grads, left, right)


def copies(value, count):
    return jnp.broadcast_to(value[None], (count,) + value.shape)


def dot(left, right, contract):
    return lax.dot_general(
        left, right, ((contract[:1], contract[1:]), ((), ())), preferred_element_type=jnp.float32
    )


def on_device(grad_parts, assign, left_basis, right_basis, left_stat, right_stat, moment, second):
    row_index = lax.axis_index("dp")
    owner = lax.axis_index("owner")
    dp_num = lax.axis_size("dp")
    owner_num = lax.axis_size("owner")
    col_num = grad_parts.shape[3]
    row_num = col_num // dp_num
    slot_cap = left_basis.shape[1]
    chunk_num = col_num // LANES
    chips = dp_num // 2
    chip = row_index // 2
    first = row_index % 2 == 0
    chip_rows = 2 * row_num
    z_num = owner_num // 2
    z = owner // 2
    kinds = 2

    came = swap_cores(
        first_payload((row_index % 2).reshape(1), grad_parts, left_basis, right_basis)
    )
    numbers = slot_numbers(assign)
    chip_grads = jnp.stack(
        [grad_parts.reshape(chips, chip_rows, col_num), came.reshape(chips, chip_rows, col_num)], 1
    ).reshape(chips, 2 * chip_rows, col_num)
    slots = jnp.stack([left_basis[0], right_basis[0]], 1)
    slot_rows = slot_cap * kinds * row_num
    chip_slots = jnp.stack([came[:slot_rows].reshape(slots.shape), slots], 2)
    chip_slots = chip_slots.reshape(slot_cap, kinds * chip_rows, col_num)
    code = numbers[:, None, None]
    picked = chip_slots[0][None]
    for slot in range(1, slot_cap):
        picked = jnp.where(code == slot, chip_slots[slot][None], picked)

    parts = exchange(jnp.where(first, chip_grads, picked))
    grad_rows = jnp.sum(
        parts.reshape(2 * chips, chip_rows, col_num).astype(jnp.float32), axis=0
    ).astype(half)
    home = lax.dynamic_index_in_dim(parts, assign[owner], 0, keepdims=False)

    states = jnp.stack([moment[0], second[0]], 1).astype(half)
    states, came = lax.optimization_barrier((states, came))
    beside = swap_owners(states)
    owner_x = owner % 2
    from_owner = lax.dynamic_index_in_dim(assign.reshape(z_num, 2), owner_x, 1, keepdims=False)
    number = lax.dynamic_index_in_dim(numbers.reshape(z_num, 2), owner_x, 1, keepdims=False)
    code = number + slot_cap * (from_owner % 2 != owner_x)
    code = z_order(code, z)[:, None, None, None]
    states = jnp.concatenate([states, beside], 0)
    picked = states[0][None]
    for slot in range(1, 2 * slot_cap):
        picked = jnp.where(code == slot, states[slot][None], picked)
    picked, home = lax.optimization_barrier((picked, home))
    states = picked[0]
    distance = (z - assign[owner] // 2) % z_num
    for step in range(1, z_num):
        states = jnp.where(distance == step, shift_z(picked[step], step), states)

    left_rows, right_rows = home.reshape(kinds, chip_rows, col_num)
    left_chunks = left_rows.reshape(chip_rows, chunk_num, LANES).transpose(1, 0, 2)
    left_chunks = jnp.broadcast_to(
        left_chunks[:, None], (chunk_num, chips // chunk_num, chip_rows, LANES)
    ).reshape(chips, chip_rows, LANES)
    rows = copies(jnp.where(first, grad_rows, right_rows), chips)
    mine = exchange_dp(jnp.concatenate([rows, left_chunks], 2))
    mine = mine.reshape(col_num, col_num + LANES)

    extra = jnp.concatenate([left_rows, states.reshape(-1, col_num)], 0)
    extra = jnp.concatenate([extra, extra[:, :LANES]], 1)
    other = swap_cores(jnp.concatenate([mine, extra], 0))
    left_rows = other[col_num : col_num + chip_rows, :col_num]
    other_states = other[col_num + chip_rows :, :col_num].reshape(states.shape)
    states = jnp.concatenate([states, other_states], 1).astype(jnp.float32)
    other = other[:col_num]
    core_full = mine[:, :col_num]
    grad_full = jnp.where(first, core_full, other[:, :col_num])
    right_full = jnp.where(first, other[:, :col_num], core_full)
    left_cols = jnp.where(first, other[:, col_num:], mine[:, col_num:])

    chunk = row_index // (dp_num // chunk_num)
    in_chunk = (row_index % (dp_num // chunk_num)) * row_num
    grad_cols = lax.dynamic_slice_in_dim(grad_full, chunk * LANES, LANES, 1)
    grad_rows = lax.dynamic_slice_in_dim(grad_full, row_index * row_num, row_num, 0)
    left_term = dot(grad_rows, grad_full, (1, 1)).astype(half)
    right_term = dot(grad_cols, grad_full, (0, 0)).astype(half)
    right_term = lax.dynamic_slice_in_dim(right_term, in_chunk, row_num, 0)
    grams = jnp.stack([left_term, right_term])
    beside = swap_owners(grams)
    grams = jnp.where(
        owner_x == 0, jnp.stack([grams, beside], 0), jnp.stack([beside, grams], 0)
    )

    in_chunk = (chip % (chips // chunk_num)) * chip_rows
    turned = dot(left_cols, grad_full, (0, 0)).astype(half)
    turned = lax.dynamic_slice_in_dim(turned, in_chunk, chip_rows, 0)
    rotated = dot(turned, right_full, (1, 0))
    home_moment = beta_one * states[0] + (1.0 - beta_one) * rotated
    home_second = beta_two * states[1] + (1.0 - beta_two) * rotated * rotated
    direction = (home_moment / bias_one / (jnp.sqrt(home_second / bias_two) + adam_eps)).astype(half)
    back_rows = dot(direction, right_full, (1, 1)).astype(half)

    results = copies(jnp.where(first, back_rows, rotated.astype(half)), chips)
    results, grams = lax.optimization_barrier((results, grams))
    gathered = exchange(results)

    held = (assign == owner)[None, :] & (
        numbers[None, :] == jnp.arange(slot_cap, dtype=jnp.int32)[:, None]
    )
    held_z = held.reshape(slot_cap, z_num, 2)
    behind = lax.dynamic_slice_in_dim(
        jnp.concatenate([held_z[:, ::-1], held_z[:, ::-1]], 1), z_num - 1 - z, z_num, 1
    )
    all_grams = [grams] + [shift_z(grams, step) for step in range(1, z_num)]
    slot_grams = jnp.zeros((slot_cap,) + grams.shape[1:], half)
    for step, values in enumerate(all_grams):
        for x in range(2):
            mask = behind[:, step, x][:, None, None, None]
            slot_grams = jnp.where(mask, values[x][None], slot_grams)
    slot_grams = slot_grams.astype(jnp.float32)

    back_full = gathered.reshape(col_num, col_num)
    chip_update = dot(left_rows, back_full, (1, 0)).astype(half)
    turns = jnp.where(held[:, :, None, None], gathered[None].astype(jnp.float32), 0.0)
    turns = jnp.sum(turns, axis=1).astype(half).reshape(slot_cap, 2, row_num, col_num)
    for_second = jnp.concatenate([chip_update[row_num:], turns[1:, 0].reshape(-1, col_num)], 0)
    came = swap_cores(jnp.where(first, for_second, turns[:, 0].reshape(-1, col_num)))
    update = jnp.where(first, chip_update[:row_num], came[:row_num])
    turns = jnp.where(first, came.reshape(turns[:, 0].shape), turns[:, 1]).astype(jnp.float32)

    new_left = beta_two * left_stat[0] + (1.0 - beta_two) * slot_grams[:, 0]
    new_right = beta_two * right_stat[0] + (1.0 - beta_two) * slot_grams[:, 1]
    new_moment = beta_one * moment[0] + (1.0 - beta_one) * turns
    new_second = beta_two * second[0] + (1.0 - beta_two) * turns * turns
    return (update[None], new_left[None], new_right[None], new_moment[None], new_second[None])


def solution(mesh):
    placed = (
        P("dp", "owner", None, None),
        P(),
        P("owner", None, "dp", None),
        P("owner", None, "dp", None),
        P("owner", None, "dp", None),
        P("owner", None, "dp", None),
        P("owner", None, "dp", None),
        P("owner", None, "dp", None),
    )
    return jax.shard_map(
        on_device,
        mesh=mesh,
        in_specs=placed,
        out_specs=(
            P("owner", "dp", None),
            P("owner", None, "dp", None),
            P("owner", None, "dp", None),
            P("owner", None, "dp", None),
            P("owner", None, "dp", None),
        ),
        check_vma=False,
    )
```

```python
import jax
import jax.numpy as jnp
from jax import lax
from jax.experimental import pallas as pl
from jax.experimental.pallas import tpu as pltpu
from jax.sharding import PartitionSpec as P

beta_one = 0.9
beta_two = 0.95
step_count = 10.0
adam_eps = 1e-08
bias_one = 1.0 - beta_one**step_count
bias_two = 1.0 - beta_two**step_count

LANES = 128
half = jnp.bfloat16


def slot_numbers(assign):
    positions = jnp.arange(assign.shape[0], dtype=jnp.int32)
    matching = assign[:, None] == assign[None, :]
    earlier = positions[None, :] < positions[:, None]
    return jnp.sum((matching & earlier).astype(jnp.int32), axis=1)


def swap_cores(value):
    return lax.ppermute(value, "dp", [(i, i ^ 1) for i in range(lax.axis_size("dp"))])


def place(chip, core, owner):
    return (chip * 2 + core) * lax.axis_size("owner") + owner


def exchange_dp(pieces):
    chips = lax.axis_size("dp") // 2
    groups = [[chip * 2 + core for chip in range(chips)] for core in range(2)]
    return lax.all_to_all(pieces, "dp", 0, 0, axis_index_groups=groups)


def exchange(pieces):
    chips = lax.axis_size("dp") // 2
    owners = lax.axis_size("owner")
    groups = [[place(chip, 0, owner) for chip in range(chips)] for owner in range(owners)]
    groups += [[place(chip, 1, owner) for owner in range(owners)] for chip in range(chips)]
    return lax.all_to_all(pieces, ("dp", "owner"), 0, 0, axis_index_groups=groups)


def swap_owners(value, bit):
    return lax.ppermute(value, "owner", [(i, i ^ bit) for i in range(lax.axis_size("owner"))])


def halve(held, owner_z, z, step):
    bit = (z >> step) % 2
    pick = lambda value, index: lax.index_in_dim(value, index, 0, keepdims=False)
    keep = jnp.where(bit == 0, pick(held, 0), pick(held, 1))
    send = jnp.where(bit == 0, pick(held, 1), pick(held, 0))
    owner_z = jnp.where(bit == 0, pick(owner_z, 0), pick(owner_z, 1))
    came = swap_owners(send, 2 << step)
    mask = ((owner_z >> step) % 2) == bit
    mask = mask.reshape(mask.shape + (1,) * (keep.ndim - mask.ndim))
    return jnp.where(mask, keep, came), owner_z


def first_payload_kernel(core, grads, left, right, payload, sems):
    slot_cap, row_num = left.shape[1:3]

    @pl.when(core[0] == 0)
    def _():
        moves = []
        for slot in range(slot_cap):
            for kind, basis in enumerate((left, right)):
                place_of = slot * 2 + kind
                moves.append(
                    pltpu.make_async_copy(
                        basis.at[0, slot],
                        payload.at[pl.ds(place_of * row_num, row_num)],
                        sems.at[place_of],
                    )
                )
        for move in moves:
            move.start()
        for move in moves:
            move.wait()

    @pl.when(core[0] != 0)
    def _():
        move = pltpu.make_async_copy(grads.at[0, 0], payload, sems.at[0])
        move.start()
        move.wait()


def first_payload(core, grads, left, right):
    anywhere = pl.BlockSpec(memory_space=pl.ANY)
    return pl.pallas_call(
        first_payload_kernel,
        out_shape=jax.ShapeDtypeStruct(grads.shape[2:], half),
        in_specs=[pl.BlockSpec(memory_space=pltpu.SMEM)] + [anywhere] * 3,
        out_specs=pl.BlockSpec(memory_space=pltpu.VMEM),
        scratch_shapes=[pltpu.SemaphoreType.DMA((2 * left.shape[1],))],
        compiler_params=pltpu.CompilerParams(vmem_limit_bytes=60 * 1024 * 1024),
        name="first_payload",
    )(core, grads, left, right)


def copies(value, count):
    return jnp.broadcast_to(value[None], (count,) + value.shape)


def dot(left, right, contract):
    return lax.dot_general(
        left, right, ((contract[:1], contract[1:]), ((), ())), preferred_element_type=jnp.float32
    )


def on_device(grad_parts, assign, left_basis, right_basis, left_stat, right_stat, moment, second):
    row_index = lax.axis_index("dp")
    owner = lax.axis_index("owner")
    dp_num = lax.axis_size("dp")
    owner_num = lax.axis_size("owner")
    col_num = grad_parts.shape[3]
    row_num = col_num // dp_num
    slot_cap = left_basis.shape[1]
    chunk_num = col_num // LANES
    chips = dp_num // 2
    chip = row_index // 2
    first = row_index % 2 == 0
    chip_rows = 2 * row_num
    z_num = owner_num // 2
    z = owner // 2
    kinds = 2

    came = swap_cores(
        first_payload((row_index % 2).reshape(1), grad_parts, left_basis, right_basis)
    )
    numbers = slot_numbers(assign)
    chip_grads = jnp.stack(
        [grad_parts.reshape(chips, chip_rows, col_num), came.reshape(chips, chip_rows, col_num)], 1
    ).reshape(chips, 2 * chip_rows, col_num)
    slots = jnp.stack([left_basis[0], right_basis[0]], 1)
    slot_rows = slot_cap * kinds * row_num
    chip_slots = jnp.stack([came[:slot_rows].reshape(slots.shape), slots], 2)
    chip_slots = chip_slots.reshape(slot_cap, kinds * chip_rows, col_num)
    code = numbers[:, None, None]
    picked = chip_slots[0][None]
    for slot in range(1, slot_cap):
        picked = jnp.where(code == slot, chip_slots[slot][None], picked)

    parts = exchange(jnp.where(first, chip_grads, picked))
    grad_rows = jnp.sum(
        parts.reshape(2 * chips, chip_rows, col_num).astype(jnp.float32), axis=0
    ).astype(half)
    home = lax.dynamic_index_in_dim(parts, assign[owner], 0, keepdims=False)

    states = jnp.stack([moment[0], second[0]], 1).astype(half)
    states, came = lax.optimization_barrier((states, came))
    beside = swap_owners(states, 1)
    owner_x = owner % 2
    from_owner = lax.dynamic_index_in_dim(assign.reshape(z_num, 2), owner_x, 1, keepdims=False)
    number = lax.dynamic_index_in_dim(numbers.reshape(z_num, 2), owner_x, 1, keepdims=False)
    code = (number + slot_cap * (from_owner % 2 != owner_x))[:, None, None, None]
    states = jnp.concatenate([states, beside], 0)
    picked = states[0][None]
    for slot in range(1, 2 * slot_cap):
        picked = jnp.where(code == slot, states[slot][None], picked)
    states = picked.reshape((2, 2, 2) + picked.shape[1:]).transpose(2, 1, 0, 3, 4, 5)
    owner_z = (from_owner // 2).reshape(2, 2, 2).transpose(2, 1, 0)
    states, owner_z = halve(states, owner_z, z, 0)
    states, home = lax.optimization_barrier((states, home))
    states, owner_z = halve(states, owner_z, z, 1)
    states, owner_z = halve(states, owner_z, z, 2)

    left_rows, right_rows = home.reshape(kinds, chip_rows, col_num)
    left_chunks = left_rows.reshape(chip_rows, chunk_num, LANES).transpose(1, 0, 2)
    left_chunks = jnp.broadcast_to(
        left_chunks[:, None], (chunk_num, chips // chunk_num, chip_rows, LANES)
    ).reshape(chips, chip_rows, LANES)
    rows = copies(jnp.where(first, grad_rows, right_rows), chips)
    mine = exchange_dp(jnp.concatenate([rows, left_chunks], 2))
    mine = mine.reshape(col_num, col_num + LANES)

    extra = jnp.concatenate([left_rows, states.reshape(-1, col_num)], 0)
    extra = jnp.concatenate([extra, extra[:, :LANES]], 1)
    other = swap_cores(jnp.concatenate([mine, extra], 0))
    left_rows = other[col_num : col_num + chip_rows, :col_num]
    other_states = other[col_num + chip_rows :, :col_num].reshape(states.shape)
    states = jnp.concatenate([states, other_states], 1).astype(jnp.float32)
    other = other[:col_num]
    core_full = mine[:, :col_num]
    grad_full = jnp.where(first, core_full, other[:, :col_num])
    right_full = jnp.where(first, other[:, :col_num], core_full)
    left_cols = jnp.where(first, other[:, col_num:], mine[:, col_num:])

    chunk = chip // (chips // chunk_num)
    in_chunk = (chip % (chips // chunk_num)) * chip_rows
    own_rows = lambda value: lax.dynamic_slice_in_dim(value, in_chunk, chip_rows, 0)
    turned = own_rows(dot(left_cols, grad_full, (0, 0)).astype(half))
    rotated = dot(turned, right_full, (1, 0))
    home_moment = beta_one * states[0] + (1.0 - beta_one) * rotated
    home_second = beta_two * states[1] + (1.0 - beta_two) * rotated * rotated
    direction = (home_moment / bias_one / (jnp.sqrt(home_second / bias_two) + adam_eps)).astype(half)
    back_rows = dot(direction, right_full, (1, 1)).astype(half)
    grad_cols = lax.dynamic_slice_in_dim(grad_full, chunk * LANES, LANES, 1)
    grad_rows = lax.dynamic_slice_in_dim(grad_full, chip * chip_rows, chip_rows, 0)
    left_term = dot(grad_rows, grad_full, (1, 1)).astype(half)
    right_term = own_rows(dot(grad_cols, grad_full, (0, 0)).astype(half))

    results = jnp.concatenate(
        [jnp.where(first, back_rows, left_term), right_term, rotated.astype(half)], 0
    )
    gathered = exchange(copies(results, chips))
    back_full = gathered[:, :chip_rows].reshape(col_num, col_num)
    chip_update = dot(left_rows, back_full, (1, 0)).astype(half)
    held = (assign == owner)[None, :] & (
        numbers[None, :] == jnp.arange(slot_cap, dtype=jnp.int32)[:, None]
    )
    chip_results = jnp.sum(
        jnp.where(held[:, :, None, None], gathered[None].astype(jnp.float32), 0.0), axis=1
    ).astype(half)
    chip_results = chip_results.reshape(slot_cap, 3, 2, row_num, col_num)
    for_first = chip_results[:, :, 0].reshape(-1, col_num)
    for_second = jnp.concatenate([chip_update[row_num:], for_first[row_num:]], 0)
    came = swap_cores(jnp.where(first, for_second, for_first))
    update = jnp.where(first, chip_update[:row_num], came[:row_num])
    terms = jnp.where(
        first, came.reshape(slot_cap, 3, row_num, col_num), chip_results[:, :, 1]
    ).astype(jnp.float32)

    new_left = beta_two * left_stat[0] + (1.0 - beta_two) * terms[:, 0]
    new_right = beta_two * right_stat[0] + (1.0 - beta_two) * terms[:, 1]
    new_moment = beta_one * moment[0] + (1.0 - beta_one) * terms[:, 2]
    new_second = beta_two * second[0] + (1.0 - beta_two) * terms[:, 2] * terms[:, 2]
    return (update[None], new_left[None], new_right[None], new_moment[None], new_second[None])


def solution(mesh):
    placed = (
        P("dp", "owner", None, None),
        P(),
        P("owner", None, "dp", None),
        P("owner", None, "dp", None),
        P("owner", None, "dp", None),
        P("owner", None, "dp", None),
        P("owner", None, "dp", None),
        P("owner", None, "dp", None),
    )
    return jax.shard_map(
        on_device,
        mesh=mesh,
        in_specs=placed,
        out_specs=(
            P("owner", "dp", None),
            P("owner", None, "dp", None),
            P("owner", None, "dp", None),
            P("owner", None, "dp", None),
            P("owner", None, "dp", None),
        ),
        check_vma=False,
    )
```

```python
import jax
import jax.numpy as jnp
from jax import lax
from jax.experimental import pallas as pl
from jax.experimental.pallas import tpu as pltpu
from jax.sharding import PartitionSpec as P

beta_one = 0.9
beta_two = 0.95
step_count = 10.0
adam_eps = 1e-08
bias_one = 1.0 - beta_one**step_count
bias_two = 1.0 - beta_two**step_count

LANES = 128
half = jnp.bfloat16


def slot_numbers(assign):
    positions = jnp.arange(assign.shape[0], dtype=jnp.int32)
    matching = assign[:, None] == assign[None, :]
    earlier = positions[None, :] < positions[:, None]
    return jnp.sum((matching & earlier).astype(jnp.int32), axis=1)


def swap_cores(value):
    return lax.ppermute(value, "dp", [(i, i ^ 1) for i in range(lax.axis_size("dp"))])


def place(chip, core, owner):
    return (chip * 2 + core) * lax.axis_size("owner") + owner


def exchange_dp(pieces):
    chips = lax.axis_size("dp") // 2
    groups = [[chip * 2 + core for chip in range(chips)] for core in range(2)]
    return lax.all_to_all(pieces, "dp", 0, 0, axis_index_groups=groups)


def exchange(pieces):
    chips = lax.axis_size("dp") // 2
    owners = lax.axis_size("owner")
    groups = [[place(chip, 0, owner) for chip in range(chips)] for owner in range(owners)]
    groups += [[place(chip, 1, owner) for owner in range(owners)] for chip in range(chips)]
    return lax.all_to_all(pieces, ("dp", "owner"), 0, 0, axis_index_groups=groups)


def exchange_lines(pieces, y_core):
    chips = lax.axis_size("dp") // 2
    owners = lax.axis_size("owner")
    groups = [
        [place(2 * y + x, y_core, owner) for y in range(chips // 2)]
        for owner in range(owners)
        for x in range(2)
    ]
    groups += [
        [place(chip, 1 - y_core, 2 * z + x) for z in range(owners // 2)]
        for chip in range(chips)
        for x in range(2)
    ]
    return lax.all_to_all(pieces, ("dp", "owner"), 0, 0, axis_index_groups=groups)


def swap_x(value):
    chips = lax.axis_size("dp") // 2
    owners = lax.axis_size("owner")
    pairs = []
    for chip in range(chips):
        for owner in range(owners):
            pairs.append((place(chip, 0, owner), place(chip ^ 1, 0, owner)))
            pairs.append((place(chip, 1, owner), place(chip, 1, owner ^ 1)))
    return lax.ppermute(value, ("dp", "owner"), pairs)


def swap_owners_first(value):
    chips = lax.axis_size("dp") // 2
    owners = lax.axis_size("owner")
    pairs = [
        (place(chip, 0, owner), place(chip, 0, owner ^ 1))
        for chip in range(chips)
        for owner in range(owners)
    ]
    return lax.ppermute(value, ("dp", "owner"), pairs)


def first_payload_kernel(core, grads, left, right, moment, second, payload, wide, sems):
    slot_cap, row_num = left.shape[1:3]

    @pl.when(core[0] == 0)
    def _():
        moves = []
        for slot in range(slot_cap):
            for kind, basis in enumerate((left, right)):
                moves.append(
                    pltpu.make_async_copy(
                        basis.at[0, slot],
                        payload.at[pl.ds((slot * 4 + kind) * row_num, row_num)],
                        sems.at[slot * 2 + kind],
                    )
                )
        for kind, state in enumerate((moment, second)):
            moves.append(
                pltpu.make_async_copy(
                    state.at[0], wide.at[kind], sems.at[2 * slot_cap + kind]
                )
            )
        for move in moves:
            move.start()
        for move in moves:
            move.wait()
        for slot in range(slot_cap):
            for kind in range(2):
                payload[pl.ds((slot * 4 + 2 + kind) * row_num, row_num)] = wide[
                    kind, slot
                ].astype(half)

    @pl.when(core[0] != 0)
    def _():
        move = pltpu.make_async_copy(grads.at[0, 0], payload, sems.at[0])
        move.start()
        move.wait()


def first_payload(core, grads, left, right, moment, second):
    slot_cap, row_num, col_num = left.shape[1:]
    anywhere = pl.BlockSpec(memory_space=pl.ANY)
    return pl.pallas_call(
        first_payload_kernel,
        out_shape=jax.ShapeDtypeStruct(grads.shape[2:], half),
        in_specs=[pl.BlockSpec(memory_space=pltpu.SMEM)] + [anywhere] * 5,
        out_specs=pl.BlockSpec(memory_space=pltpu.VMEM),
        scratch_shapes=[
            pltpu.VMEM((2, slot_cap, row_num, col_num), jnp.float32),
            pltpu.SemaphoreType.DMA((2 * slot_cap + 2,)),
        ],
        compiler_params=pltpu.CompilerParams(vmem_limit_bytes=60 * 1024 * 1024),
        name="first_payload",
    )(core, grads, left, right, moment, second)


def copies(value, count):
    return jnp.broadcast_to(value[None], (count,) + value.shape)


def dot(left, right, contract):
    return lax.dot_general(
        left, right, ((contract[:1], contract[1:]), ((), ())), preferred_element_type=jnp.float32
    )


def on_device(grad_parts, assign, left_basis, right_basis, left_stat, right_stat, moment, second):
    row_index = lax.axis_index("dp")
    owner = lax.axis_index("owner")
    dp_num = lax.axis_size("dp")
    owner_num = lax.axis_size("owner")
    col_num = grad_parts.shape[3]
    row_num = col_num // dp_num
    slot_cap = left_basis.shape[1]
    chunk_num = col_num // LANES
    chips = dp_num // 2
    chip = row_index // 2
    first = row_index % 2 == 0
    chip_rows = 2 * row_num
    kinds = 4

    grads = grad_parts[0, 0]
    came = swap_cores(
        first_payload(
            (row_index % 2).reshape(1), grad_parts, left_basis, right_basis, moment, second
        )
    )
    slots = jnp.stack(
        [left_basis[0], right_basis[0], moment[0].astype(half), second[0].astype(half)], 1
    )
    numbers = slot_numbers(assign)

    y_num = chips // 2
    z_num = owner_num // 2
    pair = (grads.astype(jnp.float32) + came.astype(jnp.float32)).astype(half)
    pair = pair.reshape(y_num, 2, chip_rows, col_num)
    even = chip % 2 == 0
    kept = jnp.where(even, pair[:, 0], pair[:, 1])
    sent = jnp.where(even, pair[:, 1], pair[:, 0]).reshape(-1, col_num)
    slot_rows = slot_cap * kinds * row_num
    chip_slots = jnp.stack([came[:slot_rows].reshape(slots.shape), slots], 2)
    chip_slots = chip_slots.reshape(slot_cap * kinds * chip_rows, col_num)
    sent_num = sent.shape[0]
    beside = swap_x(
        jnp.concatenate(
            [jnp.where(first, sent, chip_slots[:sent_num]), chip_slots[sent_num:]], 0
        )
    )
    sums = kept.astype(jnp.float32) + beside[:sent_num].reshape(kept.shape).astype(jnp.float32)
    sums = sums.astype(half)

    owner_x = owner % 2
    from_owner = lax.dynamic_index_in_dim(assign.reshape(z_num, 2), owner_x, 1, keepdims=False)
    number = lax.dynamic_index_in_dim(numbers.reshape(z_num, 2), owner_x, 1, keepdims=False)
    code = (number + slot_cap * (from_owner % 2 != owner_x))[:, None, None]
    chip_slots = chip_slots.reshape(slot_cap, kinds * chip_rows, col_num)
    beside = beside.reshape(chip_slots.shape)
    picked = chip_slots[0][None]
    for slot in range(1, slot_cap):
        picked = jnp.where(code == slot, chip_slots[slot][None], picked)
    for slot in range(slot_cap):
        picked = jnp.where(code == slot_cap + slot, beside[slot][None], picked)

    parts = exchange_lines(
        jnp.concatenate(
            [jnp.where(first, sums, picked[:, :chip_rows]), picked[:, chip_rows:]], 1
        ),
        0,
    )
    grad_rows = jnp.sum(parts[:, :chip_rows].astype(jnp.float32), axis=0).astype(half)
    home = lax.dynamic_index_in_dim(parts, assign[owner] // 2, 0, keepdims=False)

    left_rows, right_rows = home.reshape(kinds, chip_rows, col_num)[:2]
    left_chunks = left_rows.reshape(chip_rows, chunk_num, LANES).transpose(1, 0, 2)
    left_chunks = jnp.broadcast_to(
        left_chunks[:, None], (chunk_num, chips // chunk_num, chip_rows, LANES)
    ).reshape(chips, chip_rows, LANES)
    rows = copies(jnp.where(first, grad_rows, right_rows), chips)
    mine = exchange_dp(jnp.concatenate([rows, left_chunks], 2))
    mine = mine.reshape(col_num, col_num + LANES)

    chunk = chip // (chips // chunk_num)
    in_chunk = (chip % (chips // chunk_num)) * chip_rows
    own_rows = lambda value: lax.dynamic_slice_in_dim(value, in_chunk, chip_rows, 0)
    core_full = mine[:, :col_num]
    grad_cols = lax.dynamic_slice_in_dim(core_full, chunk * LANES, LANES, 1)
    left_term = dot(grad_rows, core_full, (1, 1)).astype(half)
    right_term = own_rows(dot(grad_cols, core_full, (0, 0)).astype(half))
    grams = exchange_lines(copies(jnp.concatenate([left_term, right_term], 0), z_num), 1)

    wide_home = jnp.concatenate([home, home[:, :LANES]], 1)
    other = swap_cores(jnp.concatenate([mine, wide_home], 0))
    home = jnp.where(first, other[col_num:, :col_num], home).reshape(kinds, chip_rows, col_num)
    other = other[:col_num]
    grad_full = jnp.where(first, core_full, other[:, :col_num])
    right_full = jnp.where(first, other[:, :col_num], core_full)
    left_cols = jnp.where(first, other[:, col_num:], mine[:, col_num:])

    turned = own_rows(dot(left_cols, grad_full, (0, 0)).astype(half))
    rotated = dot(turned, right_full, (1, 0))
    home_moment = beta_one * home[2].astype(jnp.float32) + (1.0 - beta_one) * rotated
    home_second = beta_two * home[3].astype(jnp.float32) + (1.0 - beta_two) * rotated * rotated
    direction = (home_moment / bias_one / (jnp.sqrt(home_second / bias_two) + adam_eps)).astype(half)
    back_rows = dot(direction, right_full, (1, 1)).astype(half)

    results = copies(jnp.where(first, back_rows, rotated.astype(half)), chips)
    results, grams = lax.optimization_barrier((results, grams))
    gathered = exchange(results)
    held = lambda blocks, counts, target: (blocks == target)[None, :] & (
        counts[None, :] == jnp.arange(slot_cap, dtype=jnp.int32)[:, None]
    )

    def taken(mask, values):
        values = jnp.where(mask[:, :, None, None], values[None].astype(jnp.float32), 0.0)
        return jnp.sum(values, axis=1).astype(half)

    own_grams = taken(held(from_owner, number, owner), grams)
    beside_grams = taken(held(from_owner, number, owner ^ 1), grams)
    own_grams = own_grams + swap_owners_first(beside_grams)
    own_grams = own_grams.reshape(slot_cap * 2, 2, row_num, col_num)

    back_full = gathered.reshape(col_num, col_num)
    chip_update = dot(home[0], back_full, (1, 0)).astype(half)
    turns = taken(held(assign, numbers, owner), gathered).reshape(slot_cap, 2, row_num, col_num)
    for_second = jnp.concatenate(
        [chip_update[row_num:], own_grams[:, 1].reshape(-1, col_num)], 0
    )
    turn_rows = slot_cap * row_num
    for_first = jnp.where(first, for_second[:turn_rows], turns[:, 0].reshape(-1, col_num))
    came = swap_cores(jnp.concatenate([for_first, for_second[turn_rows:]], 0))
    update = jnp.where(first, chip_update[:row_num], came[:row_num])
    grams = jnp.where(first, own_grams[:, 0], came[row_num:].reshape(own_grams[:, 0].shape))
    grams = grams.reshape(slot_cap, 2, row_num, col_num).astype(jnp.float32)
    turns = jnp.where(first, came[:turn_rows].reshape(turns[:, 0].shape), turns[:, 1])
    turns = turns.astype(jnp.float32)

    new_left = beta_two * left_stat[0] + (1.0 - beta_two) * grams[:, 0]
    new_right = beta_two * right_stat[0] + (1.0 - beta_two) * grams[:, 1]
    new_moment = beta_one * moment[0] + (1.0 - beta_one) * turns
    new_second = beta_two * second[0] + (1.0 - beta_two) * turns * turns
    return (update[None], new_left[None], new_right[None], new_moment[None], new_second[None])


def solution(mesh):
    placed = (
        P("dp", "owner", None, None),
        P(),
        P("owner", None, "dp", None),
        P("owner", None, "dp", None),
        P("owner", None, "dp", None),
        P("owner", None, "dp", None),
        P("owner", None, "dp", None),
        P("owner", None, "dp", None),
    )
    return jax.shard_map(
        on_device,
        mesh=mesh,
        in_specs=placed,
        out_specs=(
            P("owner", "dp", None),
            P("owner", None, "dp", None),
            P("owner", None, "dp", None),
            P("owner", None, "dp", None),
            P("owner", None, "dp", None),
        ),
        check_vma=False,
    )
```

```python
import jax
import jax.numpy as jnp
from jax import lax
from jax.experimental import pallas as pl
from jax.experimental.pallas import tpu as pltpu
from jax.sharding import PartitionSpec as P

beta_one = 0.9
beta_two = 0.95
step_count = 10.0
adam_eps = 1e-08
bias_one = 1.0 - beta_one**step_count
bias_two = 1.0 - beta_two**step_count

LANES = 128
half = jnp.bfloat16


def slot_numbers(assign):
    positions = jnp.arange(assign.shape[0], dtype=jnp.int32)
    matching = assign[:, None] == assign[None, :]
    earlier = positions[None, :] < positions[:, None]
    return jnp.sum((matching & earlier).astype(jnp.int32), axis=1)


def swap_cores(value):
    return lax.ppermute(value, "dp", [(i, i ^ 1) for i in range(lax.axis_size("dp"))])


def place(chip, core, owner):
    return (chip * 2 + core) * lax.axis_size("owner") + owner


def exchange_dp(pieces):
    chips = lax.axis_size("dp") // 2
    groups = [[chip * 2 + core for chip in range(chips)] for core in range(2)]
    return lax.all_to_all(pieces, "dp", 0, 0, axis_index_groups=groups)


def exchange(pieces, dp_core):
    chips = lax.axis_size("dp") // 2
    owners = lax.axis_size("owner")
    groups = [[place(chip, dp_core, owner) for chip in range(chips)] for owner in range(owners)]
    groups += [
        [place(chip, 1 - dp_core, owner) for owner in range(owners)] for chip in range(chips)
    ]
    return lax.all_to_all(pieces, ("dp", "owner"), 0, 0, axis_index_groups=groups)


def exchange_lines(pieces):
    chips = lax.axis_size("dp") // 2
    owners = lax.axis_size("owner")
    groups = [
        [place(2 * y + x, 0, owner) for y in range(chips // 2)]
        for owner in range(owners)
        for x in range(2)
    ]
    groups += [
        [place(chip, 1, 2 * z + x) for z in range(owners // 2)]
        for chip in range(chips)
        for x in range(2)
    ]
    return lax.all_to_all(pieces, ("dp", "owner"), 0, 0, axis_index_groups=groups)


def swap_x(value):
    chips = lax.axis_size("dp") // 2
    owners = lax.axis_size("owner")
    pairs = []
    for chip in range(chips):
        for owner in range(owners):
            pairs.append((place(chip, 0, owner), place(chip ^ 1, 0, owner)))
            pairs.append((place(chip, 1, owner), place(chip, 1, owner ^ 1)))
    return lax.ppermute(value, ("dp", "owner"), pairs)


def first_payload_kernel(core, grads, left, right, moment, second, payload, wide, sems):
    slot_cap, row_num = left.shape[1:3]

    @pl.when(core[0] == 0)
    def _():
        moves = []
        for slot in range(slot_cap):
            for kind, basis in enumerate((left, right)):
                moves.append(
                    pltpu.make_async_copy(
                        basis.at[0, slot],
                        payload.at[pl.ds((slot * 4 + kind) * row_num, row_num)],
                        sems.at[slot * 2 + kind],
                    )
                )
        for kind, state in enumerate((moment, second)):
            moves.append(
                pltpu.make_async_copy(
                    state.at[0], wide.at[kind], sems.at[2 * slot_cap + kind]
                )
            )
        for move in moves:
            move.start()
        for move in moves:
            move.wait()
        for slot in range(slot_cap):
            for kind in range(2):
                payload[pl.ds((slot * 4 + 2 + kind) * row_num, row_num)] = wide[
                    kind, slot
                ].astype(half)

    @pl.when(core[0] != 0)
    def _():
        move = pltpu.make_async_copy(grads.at[0, 0], payload, sems.at[0])
        move.start()
        move.wait()


def first_payload(core, grads, left, right, moment, second):
    slot_cap, row_num, col_num = left.shape[1:]
    anywhere = pl.BlockSpec(memory_space=pl.ANY)
    return pl.pallas_call(
        first_payload_kernel,
        out_shape=jax.ShapeDtypeStruct(grads.shape[2:], half),
        in_specs=[pl.BlockSpec(memory_space=pltpu.SMEM)] + [anywhere] * 5,
        out_specs=pl.BlockSpec(memory_space=pltpu.VMEM),
        scratch_shapes=[
            pltpu.VMEM((2, slot_cap, row_num, col_num), jnp.float32),
            pltpu.SemaphoreType.DMA((2 * slot_cap + 2,)),
        ],
        compiler_params=pltpu.CompilerParams(vmem_limit_bytes=60 * 1024 * 1024),
        name="first_payload",
    )(core, grads, left, right, moment, second)


def copies(value, count):
    return jnp.broadcast_to(value[None], (count,) + value.shape)


def dot(left, right, contract):
    return lax.dot_general(
        left, right, ((contract[:1], contract[1:]), ((), ())), preferred_element_type=jnp.float32
    )


def on_device(grad_parts, assign, left_basis, right_basis, left_stat, right_stat, moment, second):
    row_index = lax.axis_index("dp")
    owner = lax.axis_index("owner")
    dp_num = lax.axis_size("dp")
    owner_num = lax.axis_size("owner")
    col_num = grad_parts.shape[3]
    row_num = col_num // dp_num
    slot_cap = left_basis.shape[1]
    chunk_num = col_num // LANES
    chips = dp_num // 2
    chip = row_index // 2
    first = row_index % 2 == 0
    chip_rows = 2 * row_num
    kinds = 4

    grads = grad_parts[0, 0]
    came = swap_cores(
        first_payload(
            (row_index % 2).reshape(1), grad_parts, left_basis, right_basis, moment, second
        )
    )
    slots = jnp.stack(
        [left_basis[0], right_basis[0], moment[0].astype(half), second[0].astype(half)], 1
    )
    numbers = slot_numbers(assign)

    y_num = chips // 2
    z_num = owner_num // 2
    pair = (grads.astype(jnp.float32) + came.astype(jnp.float32)).astype(half)
    pair = pair.reshape(y_num, 2, chip_rows, col_num)
    even = chip % 2 == 0
    kept = jnp.where(even, pair[:, 0], pair[:, 1])
    sent = jnp.where(even, pair[:, 1], pair[:, 0]).reshape(-1, col_num)
    slot_rows = slot_cap * kinds * row_num
    chip_slots = jnp.stack([came[:slot_rows].reshape(slots.shape), slots], 2)
    chip_slots = chip_slots.reshape(slot_cap * kinds * chip_rows, col_num)
    sent_num = sent.shape[0]
    beside = swap_x(
        jnp.concatenate(
            [jnp.where(first, sent, chip_slots[:sent_num]), chip_slots[sent_num:]], 0
        )
    )
    sums = kept.astype(jnp.float32) + beside[:sent_num].reshape(kept.shape).astype(jnp.float32)
    sums = sums.astype(half)

    owner_x = owner % 2
    from_owner = lax.dynamic_index_in_dim(assign.reshape(z_num, 2), owner_x, 1, keepdims=False)
    number = lax.dynamic_index_in_dim(numbers.reshape(z_num, 2), owner_x, 1, keepdims=False)
    code = (number + slot_cap * (from_owner % 2 != owner_x))[:, None, None]
    chip_slots = chip_slots.reshape(slot_cap, kinds * chip_rows, col_num)
    beside = beside.reshape(chip_slots.shape)
    picked = chip_slots[0][None]
    for slot in range(1, slot_cap):
        picked = jnp.where(code == slot, chip_slots[slot][None], picked)
    for slot in range(slot_cap):
        picked = jnp.where(code == slot_cap + slot, beside[slot][None], picked)

    parts = exchange_lines(
        jnp.concatenate(
            [jnp.where(first, sums, picked[:, :chip_rows]), picked[:, chip_rows:]], 1
        )
    )
    grad_rows = jnp.sum(parts[:, :chip_rows].astype(jnp.float32), axis=0).astype(half)
    home = lax.dynamic_index_in_dim(parts, assign[owner] // 2, 0, keepdims=False)

    left_rows, right_rows = home.reshape(kinds, chip_rows, col_num)[:2]
    left_chunks = left_rows.reshape(chip_rows, chunk_num, LANES).transpose(1, 0, 2)
    left_chunks = jnp.broadcast_to(
        left_chunks[:, None], (chunk_num, chips // chunk_num, chip_rows, LANES)
    ).reshape(chips, chip_rows, LANES)
    rows = copies(jnp.where(first, grad_rows, right_rows), chips)
    mine = exchange_dp(jnp.concatenate([rows, left_chunks], 2))
    mine = mine.reshape(col_num, col_num + LANES)

    chunk = chip // (chips // chunk_num)
    in_chunk = (chip % (chips // chunk_num)) * chip_rows
    own_rows = lambda value: lax.dynamic_slice_in_dim(value, in_chunk, chip_rows, 0)
    core_full = mine[:, :col_num]
    grad_cols = lax.dynamic_slice_in_dim(core_full, chunk * LANES, LANES, 1)
    left_term = dot(grad_rows, core_full, (1, 1)).astype(half)
    right_term = own_rows(dot(grad_cols, core_full, (0, 0)).astype(half))
    grams = copies(jnp.concatenate([left_term, right_term], 0), owner_num)
    grams, home = lax.optimization_barrier((grams, home))
    grams = exchange(grams, 1)

    wide_home = jnp.concatenate([home, home[:, :LANES]], 1)
    other = swap_cores(jnp.concatenate([mine, wide_home], 0))
    home = jnp.where(first, other[col_num:, :col_num], home).reshape(kinds, chip_rows, col_num)
    other = other[:col_num]
    grad_full = jnp.where(first, core_full, other[:, :col_num])
    right_full = jnp.where(first, other[:, :col_num], core_full)
    left_cols = jnp.where(first, other[:, col_num:], mine[:, col_num:])

    turned = own_rows(dot(left_cols, grad_full, (0, 0)).astype(half))
    rotated = dot(turned, right_full, (1, 0))
    home_moment = beta_one * home[2].astype(jnp.float32) + (1.0 - beta_one) * rotated
    home_second = beta_two * home[3].astype(jnp.float32) + (1.0 - beta_two) * rotated * rotated
    direction = (home_moment / bias_one / (jnp.sqrt(home_second / bias_two) + adam_eps)).astype(half)
    back_rows = dot(direction, right_full, (1, 1)).astype(half)

    results = copies(jnp.where(first, back_rows, rotated.astype(half)), chips)
    results, grams = lax.optimization_barrier((results, grams))
    gathered = exchange(results, 0)
    held = lambda blocks, counts, target: (blocks == target)[None, :] & (
        counts[None, :] == jnp.arange(slot_cap, dtype=jnp.int32)[:, None]
    )

    def taken(mask, values):
        values = jnp.where(mask[:, :, None, None], values[None].astype(jnp.float32), 0.0)
        return jnp.sum(values, axis=1).astype(half)

    own_grams = taken(held(assign, numbers, owner), grams)
    own_grams = own_grams.reshape(slot_cap * 2, 2, row_num, col_num)

    back_full = gathered.reshape(col_num, col_num)
    chip_update = dot(home[0], back_full, (1, 0)).astype(half)
    turns = taken(held(assign, numbers, owner), gathered).reshape(slot_cap, 2, row_num, col_num)
    for_second = jnp.concatenate(
        [chip_update[row_num:], own_grams[:, 1].reshape(-1, col_num)], 0
    )
    turn_rows = slot_cap * row_num
    for_first = jnp.where(first, for_second[:turn_rows], turns[:, 0].reshape(-1, col_num))
    came = swap_cores(jnp.concatenate([for_first, for_second[turn_rows:]], 0))
    update = jnp.where(first, chip_update[:row_num], came[:row_num])
    grams = jnp.where(first, own_grams[:, 0], came[row_num:].reshape(own_grams[:, 0].shape))
    grams = grams.reshape(slot_cap, 2, row_num, col_num).astype(jnp.float32)
    turns = jnp.where(first, came[:turn_rows].reshape(turns[:, 0].shape), turns[:, 1])
    turns = turns.astype(jnp.float32)

    new_left = beta_two * left_stat[0] + (1.0 - beta_two) * grams[:, 0]
    new_right = beta_two * right_stat[0] + (1.0 - beta_two) * grams[:, 1]
    new_moment = beta_one * moment[0] + (1.0 - beta_one) * turns
    new_second = beta_two * second[0] + (1.0 - beta_two) * turns * turns
    return (update[None], new_left[None], new_right[None], new_moment[None], new_second[None])


def solution(mesh):
    placed = (
        P("dp", "owner", None, None),
        P(),
        P("owner", None, "dp", None),
        P("owner", None, "dp", None),
        P("owner", None, "dp", None),
        P("owner", None, "dp", None),
        P("owner", None, "dp", None),
        P("owner", None, "dp", None),
    )
    return jax.shard_map(
        on_device,
        mesh=mesh,
        in_specs=placed,
        out_specs=(
            P("owner", "dp", None),
            P("owner", None, "dp", None),
            P("owner", None, "dp", None),
            P("owner", None, "dp", None),
            P("owner", None, "dp", None),
        ),
        check_vma=False,
    )
```

```python
import jax
import jax.numpy as jnp
from jax import lax
from jax.experimental import pallas as pl
from jax.experimental.pallas import tpu as pltpu
from jax.sharding import PartitionSpec as P

beta_one = 0.9
beta_two = 0.95
step_count = 10.0
adam_eps = 1e-08
bias_one = 1.0 - beta_one**step_count
bias_two = 1.0 - beta_two**step_count

LANES = 128
half = jnp.bfloat16


def slot_numbers(assign):
    positions = jnp.arange(assign.shape[0], dtype=jnp.int32)
    matching = assign[:, None] == assign[None, :]
    earlier = positions[None, :] < positions[:, None]
    return jnp.sum((matching & earlier).astype(jnp.int32), axis=1)


def swap_cores(value):
    return lax.ppermute(value, "dp", [(i, i ^ 1) for i in range(lax.axis_size("dp"))])


def place(chip, core, owner):
    return (chip * 2 + core) * lax.axis_size("owner") + owner


def exchange_dp(pieces):
    chips = lax.axis_size("dp") // 2
    groups = [[chip * 2 + core for chip in range(chips)] for core in range(2)]
    return lax.all_to_all(pieces, "dp", 0, 0, axis_index_groups=groups)


def exchange_lines(pieces):
    chips = lax.axis_size("dp") // 2
    owners = lax.axis_size("owner")
    groups = [
        [place(2 * y + x, 0, owner) for y in range(chips // 2)]
        for owner in range(owners)
        for x in range(2)
    ]
    groups += [
        [place(chip, 1, 2 * z + x) for z in range(owners // 2)]
        for chip in range(chips)
        for x in range(2)
    ]
    return lax.all_to_all(pieces, ("dp", "owner"), 0, 0, axis_index_groups=groups)


def swap_x(value):
    chips = lax.axis_size("dp") // 2
    owners = lax.axis_size("owner")
    pairs = []
    for chip in range(chips):
        for owner in range(owners):
            pairs.append((place(chip, 0, owner), place(chip ^ 1, 0, owner)))
            pairs.append((place(chip, 1, owner), place(chip, 1, owner ^ 1)))
    return lax.ppermute(value, ("dp", "owner"), pairs)


def first_payload_kernel(core, grads, left, right, moment, second, payload, wide, sems):
    slot_cap, row_num = left.shape[1:3]

    @pl.when(core[0] == 0)
    def _():
        moves = []
        for slot in range(slot_cap):
            for kind, basis in enumerate((left, right)):
                moves.append(
                    pltpu.make_async_copy(
                        basis.at[0, slot],
                        payload.at[pl.ds((slot * 4 + kind) * row_num, row_num)],
                        sems.at[slot * 2 + kind],
                    )
                )
        for kind, state in enumerate((moment, second)):
            moves.append(
                pltpu.make_async_copy(
                    state.at[0], wide.at[kind], sems.at[2 * slot_cap + kind]
                )
            )
        for move in moves:
            move.start()
        for move in moves:
            move.wait()
        for slot in range(slot_cap):
            for kind in range(2):
                payload[pl.ds((slot * 4 + 2 + kind) * row_num, row_num)] = wide[
                    kind, slot
                ].astype(half)

    @pl.when(core[0] != 0)
    def _():
        move = pltpu.make_async_copy(grads.at[0, 0], payload, sems.at[0])
        move.start()
        move.wait()


def first_payload(core, grads, left, right, moment, second):
    slot_cap, row_num, col_num = left.shape[1:]
    anywhere = pl.BlockSpec(memory_space=pl.ANY)
    return pl.pallas_call(
        first_payload_kernel,
        out_shape=jax.ShapeDtypeStruct(grads.shape[2:], half),
        in_specs=[pl.BlockSpec(memory_space=pltpu.SMEM)] + [anywhere] * 5,
        out_specs=pl.BlockSpec(memory_space=pltpu.VMEM),
        scratch_shapes=[
            pltpu.VMEM((2, slot_cap, row_num, col_num), jnp.float32),
            pltpu.SemaphoreType.DMA((2 * slot_cap + 2,)),
        ],
        compiler_params=pltpu.CompilerParams(vmem_limit_bytes=60 * 1024 * 1024),
        name="first_payload",
    )(core, grads, left, right, moment, second)


def copies(value, count):
    return jnp.broadcast_to(value[None], (count,) + value.shape)


def dot(left, right, contract):
    return lax.dot_general(
        left, right, ((contract[:1], contract[1:]), ((), ())), preferred_element_type=jnp.float32
    )


def on_device(grad_parts, assign, left_basis, right_basis, left_stat, right_stat, moment, second):
    row_index = lax.axis_index("dp")
    owner = lax.axis_index("owner")
    dp_num = lax.axis_size("dp")
    owner_num = lax.axis_size("owner")
    col_num = grad_parts.shape[3]
    row_num = col_num // dp_num
    slot_cap = left_basis.shape[1]
    chunk_num = col_num // LANES
    chips = dp_num // 2
    chip = row_index // 2
    first = row_index % 2 == 0
    chip_rows = 2 * row_num
    kinds = 4

    grads = grad_parts[0, 0]
    came = swap_cores(
        first_payload(
            (row_index % 2).reshape(1), grad_parts, left_basis, right_basis, moment, second
        )
    )
    slots = jnp.stack(
        [left_basis[0], right_basis[0], moment[0].astype(half), second[0].astype(half)], 1
    )
    numbers = slot_numbers(assign)

    y_num = chips // 2
    z_num = owner_num // 2
    pair = (grads.astype(jnp.float32) + came.astype(jnp.float32)).astype(half)
    pair = pair.reshape(y_num, 2, chip_rows, col_num)
    even = chip % 2 == 0
    kept = jnp.where(even, pair[:, 0], pair[:, 1])
    sent = jnp.where(even, pair[:, 1], pair[:, 0]).reshape(-1, col_num)
    slot_rows = slot_cap * kinds * row_num
    chip_slots = jnp.stack([came[:slot_rows].reshape(slots.shape), slots], 2)
    chip_slots = chip_slots.reshape(slot_cap * kinds * chip_rows, col_num)
    sent_num = sent.shape[0]
    beside = swap_x(
        jnp.concatenate(
            [jnp.where(first, sent, chip_slots[:sent_num]), chip_slots[sent_num:]], 0
        )
    )
    sums = kept.astype(jnp.float32) + beside[:sent_num].reshape(kept.shape).astype(jnp.float32)
    sums = sums.astype(half)

    owner_x = owner % 2
    from_owner = lax.dynamic_index_in_dim(assign.reshape(z_num, 2), owner_x, 1, keepdims=False)
    number = lax.dynamic_index_in_dim(numbers.reshape(z_num, 2), owner_x, 1, keepdims=False)
    code = (number + slot_cap * (from_owner % 2 != owner_x))[:, None, None]
    chip_slots = chip_slots.reshape(slot_cap, kinds * chip_rows, col_num)
    beside = beside.reshape(chip_slots.shape)
    picked = chip_slots[0][None]
    for slot in range(1, slot_cap):
        picked = jnp.where(code == slot, chip_slots[slot][None], picked)
    for slot in range(slot_cap):
        picked = jnp.where(code == slot_cap + slot, beside[slot][None], picked)

    parts = exchange_lines(
        jnp.concatenate(
            [jnp.where(first, sums, picked[:, :chip_rows]), picked[:, chip_rows:]], 1
        )
    )
    grad_rows = jnp.sum(parts[:, :chip_rows].astype(jnp.float32), axis=0).astype(half)
    home = lax.dynamic_index_in_dim(parts, assign[owner] // 2, 0, keepdims=False)

    left_rows, right_rows = home.reshape(kinds, chip_rows, col_num)[:2]
    left_chunks = left_rows.reshape(chip_rows, chunk_num, LANES).transpose(1, 0, 2)
    left_chunks = jnp.broadcast_to(
        left_chunks[:, None], (chunk_num, chips // chunk_num, chip_rows, LANES)
    ).reshape(chips, chip_rows, LANES)
    rows = copies(jnp.where(first, grad_rows, right_rows), chips)
    mine = exchange_dp(jnp.concatenate([rows, left_chunks], 2))
    mine = mine.reshape(col_num, col_num + LANES)
    wide_home = jnp.concatenate([home, home[:, :LANES]], 1)
    other = swap_cores(jnp.concatenate([mine, wide_home], 0))
    home = jnp.where(first, other[col_num:, :col_num], home).reshape(kinds, chip_rows, col_num)
    other = other[:col_num]
    grad_full = jnp.where(first, mine[:, :col_num], other[:, :col_num])
    right_full = jnp.where(first, other[:, :col_num], mine[:, :col_num])
    left_cols = jnp.where(first, other[:, col_num:], mine[:, col_num:])

    chunk = chip // (chips // chunk_num)
    in_chunk = (chip % (chips // chunk_num)) * chip_rows
    own_rows = lambda value: lax.dynamic_slice_in_dim(value, in_chunk, chip_rows, 0)
    turned = own_rows(dot(left_cols, grad_full, (0, 0)).astype(half))
    rotated = dot(turned, right_full, (1, 0))
    home_moment = beta_one * home[2].astype(jnp.float32) + (1.0 - beta_one) * rotated
    home_second = beta_two * home[3].astype(jnp.float32) + (1.0 - beta_two) * rotated * rotated
    direction = (home_moment / bias_one / (jnp.sqrt(home_second / bias_two) + adam_eps)).astype(half)
    back_rows = dot(direction, right_full, (1, 1)).astype(half)
    grad_cols = lax.dynamic_slice_in_dim(grad_full, chunk * LANES, LANES, 1)
    chip_grad_rows = lax.dynamic_slice_in_dim(grad_full, chip * chip_rows, chip_rows, 0)
    left_term = dot(chip_grad_rows, grad_full, (1, 1)).astype(half)
    right_term = own_rows(dot(grad_cols, grad_full, (0, 0)).astype(half))

    results = jnp.concatenate(
        [jnp.where(first, back_rows, left_term), right_term, rotated.astype(half)], 0
    )
    gathered = exchange_lines(copies(results, y_num))

    def taken(target):
        mask = (from_owner == target)[None, :] & (
            number[None, :] == jnp.arange(slot_cap, dtype=jnp.int32)[:, None]
        )
        values = jnp.where(mask[:, :, None, None], gathered[None].astype(jnp.float32), 0.0)
        return jnp.sum(values, axis=1).astype(half)

    back_half = gathered[:, :chip_rows].reshape(-1, col_num)
    half_rows = back_half.shape[0]
    for_beside = taken(owner ^ 1).reshape(-1, col_num)
    beside = swap_x(
        jnp.concatenate(
            [jnp.where(first, back_half, for_beside[:half_rows]), for_beside[half_rows:]], 0
        )
    )
    chip_results = taken(owner) + beside.reshape(slot_cap, -1, col_num)
    back_half = back_half.reshape(y_num, chip_rows, col_num)
    beside = beside[:half_rows].reshape(back_half.shape)
    back_full = jnp.where(
        even, jnp.stack([back_half, beside], 1), jnp.stack([beside, back_half], 1)
    ).reshape(col_num, col_num)
    chip_update = dot(home[0], back_full, (1, 0)).astype(half)
    chip_results = chip_results.reshape(slot_cap, 3, 2, row_num, col_num)
    for_first = chip_results[:, :, 0].reshape(-1, col_num)
    for_second = jnp.concatenate([chip_update[row_num:], for_first[row_num:]], 0)
    came = swap_cores(jnp.where(first, for_second, for_first))
    update = jnp.where(first, chip_update[:row_num], came[:row_num])
    terms = jnp.where(
        first, came.reshape(slot_cap, 3, row_num, col_num), chip_results[:, :, 1]
    ).astype(jnp.float32)

    new_left = beta_two * left_stat[0] + (1.0 - beta_two) * terms[:, 0]
    new_right = beta_two * right_stat[0] + (1.0 - beta_two) * terms[:, 1]
    new_moment = beta_one * moment[0] + (1.0 - beta_one) * terms[:, 2]
    new_second = beta_two * second[0] + (1.0 - beta_two) * terms[:, 2] * terms[:, 2]
    return (update[None], new_left[None], new_right[None], new_moment[None], new_second[None])


def solution(mesh):
    placed = (
        P("dp", "owner", None, None),
        P(),
        P("owner", None, "dp", None),
        P("owner", None, "dp", None),
        P("owner", None, "dp", None),
        P("owner", None, "dp", None),
        P("owner", None, "dp", None),
        P("owner", None, "dp", None),
    )
    return jax.shard_map(
        on_device,
        mesh=mesh,
        in_specs=placed,
        out_specs=(
            P("owner", "dp", None),
            P("owner", None, "dp", None),
            P("owner", None, "dp", None),
            P("owner", None, "dp", None),
            P("owner", None, "dp", None),
        ),
        check_vma=False,
    )
```

```python
import jax
import jax.numpy as jnp
from jax import lax
from jax.experimental import pallas as pl
from jax.experimental.pallas import tpu as pltpu
from jax.sharding import PartitionSpec as P

beta_one = 0.9
beta_two = 0.95
step_count = 10.0
adam_eps = 1e-08
bias_one = 1.0 - beta_one**step_count
bias_two = 1.0 - beta_two**step_count

LANES = 128
half = jnp.bfloat16


def slot_numbers(assign):
    positions = jnp.arange(assign.shape[0], dtype=jnp.int32)
    matching = assign[:, None] == assign[None, :]
    earlier = positions[None, :] < positions[:, None]
    return jnp.sum((matching & earlier).astype(jnp.int32), axis=1)


def swap_cores(value):
    return lax.ppermute(value, "dp", [(i, i ^ 1) for i in range(lax.axis_size("dp"))])


def place(chip, core, owner):
    return (chip * 2 + core) * lax.axis_size("owner") + owner


def exchange_dp(pieces):
    chips = lax.axis_size("dp") // 2
    groups = [[chip * 2 + core for chip in range(chips)] for core in range(2)]
    return lax.all_to_all(pieces, "dp", 0, 0, axis_index_groups=groups)


def exchange_lines(pieces):
    chips = lax.axis_size("dp") // 2
    owners = lax.axis_size("owner")
    groups = [
        [place(2 * y + x, 0, owner) for y in range(chips // 2)]
        for owner in range(owners)
        for x in range(2)
    ]
    groups += [
        [place(chip, 1, 2 * z + x) for z in range(owners // 2)]
        for chip in range(chips)
        for x in range(2)
    ]
    return lax.all_to_all(pieces, ("dp", "owner"), 0, 0, axis_index_groups=groups)


def swap_x(value):
    chips = lax.axis_size("dp") // 2
    owners = lax.axis_size("owner")
    pairs = []
    for chip in range(chips):
        for owner in range(owners):
            pairs.append((place(chip, 0, owner), place(chip ^ 1, 0, owner)))
            pairs.append((place(chip, 1, owner), place(chip, 1, owner ^ 1)))
    return lax.ppermute(value, ("dp", "owner"), pairs)


def swap_across(value):
    chips = lax.axis_size("dp") // 2
    owners = lax.axis_size("owner")
    pairs = []
    for chip in range(chips):
        for owner in range(owners):
            pairs.append((place(chip, 0, owner), place(chip ^ 1, 1, owner)))
            pairs.append((place(chip, 1, owner), place(chip, 0, owner ^ 1)))
    return lax.ppermute(value, ("dp", "owner"), pairs)


def first_payload_kernel(core, grads, left, right, moment, second, payload, wide, sems):
    slot_cap, row_num = left.shape[1:3]

    @pl.when(core[0] == 0)
    def _():
        moves = []
        for slot in range(slot_cap):
            for kind, basis in enumerate((left, right)):
                moves.append(
                    pltpu.make_async_copy(
                        basis.at[0, slot],
                        payload.at[pl.ds((slot * 4 + kind) * row_num, row_num)],
                        sems.at[slot * 2 + kind],
                    )
                )
        for kind, state in enumerate((moment, second)):
            moves.append(
                pltpu.make_async_copy(
                    state.at[0], wide.at[kind], sems.at[2 * slot_cap + kind]
                )
            )
        for move in moves:
            move.start()
        for move in moves:
            move.wait()
        for slot in range(slot_cap):
            for kind in range(2):
                payload[pl.ds((slot * 4 + 2 + kind) * row_num, row_num)] = wide[
                    kind, slot
                ].astype(half)

    @pl.when(core[0] != 0)
    def _():
        move = pltpu.make_async_copy(grads.at[0, 0], payload, sems.at[0])
        move.start()
        move.wait()


def first_payload(core, grads, left, right, moment, second):
    slot_cap, row_num, col_num = left.shape[1:]
    anywhere = pl.BlockSpec(memory_space=pl.ANY)
    return pl.pallas_call(
        first_payload_kernel,
        out_shape=jax.ShapeDtypeStruct(grads.shape[2:], half),
        in_specs=[pl.BlockSpec(memory_space=pltpu.SMEM)] + [anywhere] * 5,
        out_specs=pl.BlockSpec(memory_space=pltpu.VMEM),
        scratch_shapes=[
            pltpu.VMEM((2, slot_cap, row_num, col_num), jnp.float32),
            pltpu.SemaphoreType.DMA((2 * slot_cap + 2,)),
        ],
        compiler_params=pltpu.CompilerParams(vmem_limit_bytes=60 * 1024 * 1024),
        name="first_payload",
    )(core, grads, left, right, moment, second)


def copies(value, count):
    return jnp.broadcast_to(value[None], (count,) + value.shape)


def dot(left, right, contract):
    return lax.dot_general(
        left, right, ((contract[:1], contract[1:]), ((), ())), preferred_element_type=jnp.float32
    )


def on_device(grad_parts, assign, left_basis, right_basis, left_stat, right_stat, moment, second):
    row_index = lax.axis_index("dp")
    owner = lax.axis_index("owner")
    dp_num = lax.axis_size("dp")
    owner_num = lax.axis_size("owner")
    col_num = grad_parts.shape[3]
    row_num = col_num // dp_num
    slot_cap = left_basis.shape[1]
    chunk_num = col_num // LANES
    chips = dp_num // 2
    chip = row_index // 2
    first = row_index % 2 == 0
    chip_rows = 2 * row_num
    kinds = 4

    grads = grad_parts[0, 0]
    came = swap_cores(
        first_payload(
            (row_index % 2).reshape(1), grad_parts, left_basis, right_basis, moment, second
        )
    )
    slots = jnp.stack(
        [left_basis[0], right_basis[0], moment[0].astype(half), second[0].astype(half)], 1
    )
    numbers = slot_numbers(assign)

    y_num = chips // 2
    z_num = owner_num // 2
    pair = (grads.astype(jnp.float32) + came.astype(jnp.float32)).astype(half)
    pair = pair.reshape(y_num, 2, chip_rows, col_num)
    even = chip % 2 == 0
    kept = jnp.where(even, pair[:, 0], pair[:, 1])
    sent = jnp.where(even, pair[:, 1], pair[:, 0]).reshape(-1, col_num)
    slot_rows = slot_cap * kinds * row_num
    chip_slots = jnp.stack([came[:slot_rows].reshape(slots.shape), slots], 2)
    chip_slots = chip_slots.reshape(slot_cap * kinds * chip_rows, col_num)
    sent_num = sent.shape[0]
    beside = swap_x(
        jnp.concatenate(
            [jnp.where(first, sent, chip_slots[:sent_num]), chip_slots[sent_num:]], 0
        )
    )
    sums = kept.astype(jnp.float32) + beside[:sent_num].reshape(kept.shape).astype(jnp.float32)
    sums = sums.astype(half)

    owner_x = owner % 2
    from_owner = lax.dynamic_index_in_dim(assign.reshape(z_num, 2), owner_x, 1, keepdims=False)
    number = lax.dynamic_index_in_dim(numbers.reshape(z_num, 2), owner_x, 1, keepdims=False)
    code = (number + slot_cap * (from_owner % 2 != owner_x))[:, None, None]
    chip_slots = chip_slots.reshape(slot_cap, kinds * chip_rows, col_num)
    beside = beside.reshape(chip_slots.shape)
    picked = chip_slots[0][None]
    for slot in range(1, slot_cap):
        picked = jnp.where(code == slot, chip_slots[slot][None], picked)
    for slot in range(slot_cap):
        picked = jnp.where(code == slot_cap + slot, beside[slot][None], picked)

    parts = exchange_lines(
        jnp.concatenate(
            [jnp.where(first, sums, picked[:, :chip_rows]), picked[:, chip_rows:]], 1
        )
    )
    grad_rows = jnp.sum(parts[:, :chip_rows].astype(jnp.float32), axis=0).astype(half)
    home = lax.dynamic_index_in_dim(parts, assign[owner] // 2, 0, keepdims=False)

    left_rows, right_rows = home.reshape(kinds, chip_rows, col_num)[:2]
    left_chunks = left_rows.reshape(chip_rows, chunk_num, LANES).transpose(1, 0, 2)
    left_chunks = jnp.broadcast_to(
        left_chunks[:, None], (chunk_num, chips // chunk_num, chip_rows, LANES)
    ).reshape(chips, chip_rows, LANES)
    rows = copies(jnp.where(first, grad_rows, right_rows), chips)
    mine = exchange_dp(jnp.concatenate([rows, left_chunks], 2))
    mine = mine.reshape(col_num, col_num + LANES)
    wide_home = jnp.concatenate([home, home[:, :LANES]], 1)
    other = swap_cores(jnp.concatenate([mine, wide_home], 0))
    home = jnp.where(first, other[col_num:, :col_num], home).reshape(kinds, chip_rows, col_num)
    other = other[:col_num]
    grad_full = jnp.where(first, mine[:, :col_num], other[:, :col_num])
    right_full = jnp.where(first, other[:, :col_num], mine[:, :col_num])
    left_cols = jnp.where(first, other[:, col_num:], mine[:, col_num:])

    chunk = chip // (chips // chunk_num)
    in_chunk = (chip % (chips // chunk_num)) * chip_rows
    own_rows = lambda value: lax.dynamic_slice_in_dim(value, in_chunk, chip_rows, 0)
    turned = own_rows(dot(left_cols, grad_full, (0, 0)).astype(half))
    rotated = dot(turned, right_full, (1, 0))
    home_moment = beta_one * home[2].astype(jnp.float32) + (1.0 - beta_one) * rotated
    home_second = beta_two * home[3].astype(jnp.float32) + (1.0 - beta_two) * rotated * rotated
    direction = (home_moment / bias_one / (jnp.sqrt(home_second / bias_two) + adam_eps)).astype(half)
    back_rows = dot(direction, right_full, (1, 1)).astype(half)
    grad_cols = lax.dynamic_slice_in_dim(grad_full, chunk * LANES, LANES, 1)
    chip_grad_rows = lax.dynamic_slice_in_dim(grad_full, chip * chip_rows, chip_rows, 0)
    left_term = dot(chip_grad_rows, grad_full, (1, 1)).astype(half)
    right_term = own_rows(dot(grad_cols, grad_full, (0, 0)).astype(half))

    results = jnp.concatenate(
        [jnp.where(first, back_rows, left_term), right_term, rotated.astype(half)], 0
    )
    gathered = exchange_lines(copies(results, y_num))

    def taken(target):
        mask = (from_owner == target)[None, :] & (
            number[None, :] == jnp.arange(slot_cap, dtype=jnp.int32)[:, None]
        )
        values = jnp.where(mask[:, :, None, None], gathered[None].astype(jnp.float32), 0.0)
        return jnp.sum(values, axis=1).astype(half)

    back_half = gathered[:, :chip_rows].reshape(-1, col_num)
    own = taken(owner).reshape(slot_cap, 3, 2, row_num, col_num)
    of_beside = taken(owner ^ 1).reshape(own.shape)
    result_rows = slot_cap * 3 * row_num

    def either(values):
        values = values.reshape(-1, col_num)
        return jnp.concatenate(
            [jnp.where(first, back_half[:result_rows], values), back_half[result_rows:]], 0
        )

    beside = swap_x(either(of_beside[:, :, 1]))
    across = swap_across(either(of_beside[:, :, 0]))
    came = swap_cores(either(own[:, :, 0]))
    terms = jnp.where(
        first,
        came[:result_rows] + across[:result_rows],
        own[:, :, 1].reshape(-1, col_num) + beside[:result_rows],
    )
    terms = terms.reshape(slot_cap, 3, row_num, col_num).astype(jnp.float32)
    back_half = jnp.where(first, back_half, came).reshape(y_num, chip_rows, col_num)
    beside = jnp.where(first, beside, across).reshape(back_half.shape)
    back_full = jnp.where(
        even, jnp.stack([back_half, beside], 1), jnp.stack([beside, back_half], 1)
    ).reshape(col_num, col_num)
    left_rows = jnp.where(first, home[0, :row_num], home[0, row_num:])
    update = dot(left_rows, back_full, (1, 0)).astype(half)

    new_left = beta_two * left_stat[0] + (1.0 - beta_two) * terms[:, 0]
    new_right = beta_two * right_stat[0] + (1.0 - beta_two) * terms[:, 1]
    new_moment = beta_one * moment[0] + (1.0 - beta_one) * terms[:, 2]
    new_second = beta_two * second[0] + (1.0 - beta_two) * terms[:, 2] * terms[:, 2]
    return (update[None], new_left[None], new_right[None], new_moment[None], new_second[None])


def solution(mesh):
    placed = (
        P("dp", "owner", None, None),
        P(),
        P("owner", None, "dp", None),
        P("owner", None, "dp", None),
        P("owner", None, "dp", None),
        P("owner", None, "dp", None),
        P("owner", None, "dp", None),
        P("owner", None, "dp", None),
    )
    return jax.shard_map(
        on_device,
        mesh=mesh,
        in_specs=placed,
        out_specs=(
            P("owner", "dp", None),
            P("owner", None, "dp", None),
            P("owner", None, "dp", None),
            P("owner", None, "dp", None),
            P("owner", None, "dp", None),
        ),
        check_vma=False,
    )
```

```python
import jax
import jax.numpy as jnp
from jax import lax
from jax.experimental import pallas as pl
from jax.experimental.pallas import tpu as pltpu
from jax.sharding import PartitionSpec as P

beta_one = 0.9
beta_two = 0.95
step_count = 10.0
adam_eps = 1e-08
bias_one = 1.0 - beta_one**step_count
bias_two = 1.0 - beta_two**step_count

LANES = 128
half = jnp.bfloat16


def slot_numbers(assign):
    positions = jnp.arange(assign.shape[0], dtype=jnp.int32)
    matching = assign[:, None] == assign[None, :]
    earlier = positions[None, :] < positions[:, None]
    return jnp.sum((matching & earlier).astype(jnp.int32), axis=1)


def swap_cores(value):
    return lax.ppermute(value, "dp", [(i, i ^ 1) for i in range(lax.axis_size("dp"))])


def place(chip, core, owner):
    return (chip * 2 + core) * lax.axis_size("owner") + owner


def exchange_dp(pieces):
    chips = lax.axis_size("dp") // 2
    groups = [[chip * 2 + core for chip in range(chips)] for core in range(2)]
    return lax.all_to_all(pieces, "dp", 0, 0, axis_index_groups=groups)


def exchange_lines(pieces):
    chips = lax.axis_size("dp") // 2
    owners = lax.axis_size("owner")
    groups = [
        [place(2 * y + x, 0, owner) for y in range(chips // 2)]
        for owner in range(owners)
        for x in range(2)
    ]
    groups += [
        [place(chip, 1, 2 * z + x) for z in range(owners // 2)]
        for chip in range(chips)
        for x in range(2)
    ]
    return lax.all_to_all(pieces, ("dp", "owner"), 0, 0, axis_index_groups=groups)


def swap_x(value):
    chips = lax.axis_size("dp") // 2
    owners = lax.axis_size("owner")
    pairs = []
    for chip in range(chips):
        for owner in range(owners):
            pairs.append((place(chip, 0, owner), place(chip ^ 1, 0, owner)))
            pairs.append((place(chip, 1, owner), place(chip, 1, owner ^ 1)))
    return lax.ppermute(value, ("dp", "owner"), pairs)


def first_payload_kernel(core, grads, left, right, moment, second, slots, payload, wide, sems):
    slot_cap, row_num = left.shape[1:3]
    moves = []
    for slot in range(slot_cap):
        for kind, basis in enumerate((left, right)):
            moves.append(
                pltpu.make_async_copy(
                    basis.at[0, slot], slots.at[slot, kind], sems.at[slot * 2 + kind]
                )
            )
    for kind, state in enumerate((moment, second)):
        moves.append(
            pltpu.make_async_copy(state.at[0], wide.at[kind], sems.at[2 * slot_cap + kind])
        )
    for move in moves:
        move.start()

    @pl.when(core[0] != 0)
    def _():
        move = pltpu.make_async_copy(grads.at[0, 0], payload, sems.at[2 * slot_cap + 2])
        move.start()
        move.wait()

    for move in moves:
        move.wait()
    for slot in range(slot_cap):
        for kind in range(2):
            slots[slot, 2 + kind] = wide[kind, slot].astype(half)

    @pl.when(core[0] == 0)
    def _():
        for slot in range(slot_cap):
            for kind in range(4):
                payload[pl.ds((slot * 4 + kind) * row_num, row_num)] = slots[slot, kind]


def first_payload(core, grads, left, right, moment, second):
    slot_cap, row_num, col_num = left.shape[1:]
    anywhere = pl.BlockSpec(memory_space=pl.ANY)
    vmem = pl.BlockSpec(memory_space=pltpu.VMEM)
    return pl.pallas_call(
        first_payload_kernel,
        out_shape=(
            jax.ShapeDtypeStruct((slot_cap, 4, row_num, col_num), half),
            jax.ShapeDtypeStruct(grads.shape[2:], half),
        ),
        in_specs=[pl.BlockSpec(memory_space=pltpu.SMEM)] + [anywhere] * 5,
        out_specs=(vmem, vmem),
        scratch_shapes=[
            pltpu.VMEM((2, slot_cap, row_num, col_num), jnp.float32),
            pltpu.SemaphoreType.DMA((2 * slot_cap + 3,)),
        ],
        compiler_params=pltpu.CompilerParams(vmem_limit_bytes=60 * 1024 * 1024),
        name="first_payload",
    )(core, grads, left, right, moment, second)


def copies(value, count):
    return jnp.broadcast_to(value[None], (count,) + value.shape)


def dot(left, right, contract):
    return lax.dot_general(
        left, right, ((contract[:1], contract[1:]), ((), ())), preferred_element_type=jnp.float32
    )


def on_device(grad_parts, assign, left_basis, right_basis, left_stat, right_stat, moment, second):
    row_index = lax.axis_index("dp")
    owner = lax.axis_index("owner")
    dp_num = lax.axis_size("dp")
    owner_num = lax.axis_size("owner")
    col_num = grad_parts.shape[3]
    row_num = col_num // dp_num
    slot_cap = left_basis.shape[1]
    chunk_num = col_num // LANES
    chips = dp_num // 2
    chip = row_index // 2
    first = row_index % 2 == 0
    chip_rows = 2 * row_num
    kinds = 4

    grads = grad_parts[0, 0]
    slots, payload = first_payload(
        (row_index % 2).reshape(1), grad_parts, left_basis, right_basis, moment, second
    )
    came = swap_cores(payload)

    y_num = chips // 2
    z_num = owner_num // 2
    pair = (grads.astype(jnp.float32) + came.astype(jnp.float32)).astype(half)
    pair = pair.reshape(y_num, 2, chip_rows, col_num)
    even = chip % 2 == 0
    kept = jnp.where(even, pair[:, 0], pair[:, 1])
    sent = jnp.where(even, pair[:, 1], pair[:, 0]).reshape(-1, col_num)
    slot_rows = slot_cap * kinds * row_num
    chip_slots = jnp.stack([came[:slot_rows].reshape(slots.shape), slots], 2)
    chip_slots = chip_slots.reshape(slot_cap * kinds * chip_rows, col_num)
    sent_num = sent.shape[0]
    payload = jnp.concatenate(
        [jnp.where(first, sent, chip_slots[:sent_num]), chip_slots[sent_num:]], 0
    )
    payload, assign = lax.optimization_barrier((payload, assign))
    beside = swap_x(payload)
    numbers = slot_numbers(assign)
    sums = kept.astype(jnp.float32) + beside[:sent_num].reshape(kept.shape).astype(jnp.float32)
    sums = sums.astype(half)

    owner_x = owner % 2
    from_owner = lax.dynamic_index_in_dim(assign.reshape(z_num, 2), owner_x, 1, keepdims=False)
    number = lax.dynamic_index_in_dim(numbers.reshape(z_num, 2), owner_x, 1, keepdims=False)
    code = (number + slot_cap * (from_owner % 2 != owner_x))[:, None, None]
    chip_slots = chip_slots.reshape(slot_cap, kinds * chip_rows, col_num)
    beside = beside.reshape(chip_slots.shape)
    picked = chip_slots[0][None]
    for slot in range(1, slot_cap):
        picked = jnp.where(code == slot, chip_slots[slot][None], picked)
    for slot in range(slot_cap):
        picked = jnp.where(code == slot_cap + slot, beside[slot][None], picked)

    parts = exchange_lines(
        jnp.concatenate(
            [jnp.where(first, sums, picked[:, :chip_rows]), picked[:, chip_rows:]], 1
        )
    )
    grad_rows = jnp.sum(parts[:, :chip_rows].astype(jnp.float32), axis=0).astype(half)
    home = lax.dynamic_index_in_dim(parts, assign[owner] // 2, 0, keepdims=False)

    left_rows, right_rows = home.reshape(kinds, chip_rows, col_num)[:2]
    left_chunks = left_rows.reshape(chip_rows, chunk_num, LANES).transpose(1, 0, 2)
    left_chunks = jnp.broadcast_to(
        left_chunks[:, None], (chunk_num, chips // chunk_num, chip_rows, LANES)
    ).reshape(chips, chip_rows, LANES)
    rows = copies(jnp.where(first, grad_rows, right_rows), chips)
    mine = exchange_dp(jnp.concatenate([rows, left_chunks], 2))
    mine = mine.reshape(col_num, col_num + LANES)
    wide_home = jnp.concatenate([home, home[:, :LANES]], 1)
    other = swap_cores(jnp.concatenate([mine, wide_home], 0))
    home = jnp.where(first, other[col_num:, :col_num], home).reshape(kinds, chip_rows, col_num)
    other = other[:col_num]
    grad_full = jnp.where(first, mine[:, :col_num], other[:, :col_num])
    right_full = jnp.where(first, other[:, :col_num], mine[:, :col_num])
    left_cols = jnp.where(first, other[:, col_num:], mine[:, col_num:])

    chunk = chip // (chips // chunk_num)
    in_chunk = (chip % (chips // chunk_num)) * chip_rows
    own_rows = lambda value: lax.dynamic_slice_in_dim(value, in_chunk, chip_rows, 0)
    turned = own_rows(dot(left_cols, grad_full, (0, 0)).astype(half))
    rotated = dot(turned, right_full, (1, 0))
    home_moment = beta_one * home[2].astype(jnp.float32) + (1.0 - beta_one) * rotated
    home_second = beta_two * home[3].astype(jnp.float32) + (1.0 - beta_two) * rotated * rotated
    direction = (home_moment / bias_one / (jnp.sqrt(home_second / bias_two) + adam_eps)).astype(half)
    back_rows = dot(direction, right_full, (1, 1)).astype(half)
    grad_cols = lax.dynamic_slice_in_dim(grad_full, chunk * LANES, LANES, 1)
    chip_grad_rows = lax.dynamic_slice_in_dim(grad_full, chip * chip_rows, chip_rows, 0)
    left_term = dot(chip_grad_rows, grad_full, (1, 1)).astype(half)
    right_term = own_rows(dot(grad_cols, grad_full, (0, 0)).astype(half))

    results = jnp.concatenate(
        [jnp.where(first, back_rows, left_term), right_term, rotated.astype(half)], 0
    )
    gathered = exchange_lines(copies(results, y_num))

    def taken(target):
        mask = (from_owner == target)[None, :] & (
            number[None, :] == jnp.arange(slot_cap, dtype=jnp.int32)[:, None]
        )
        values = jnp.zeros((slot_cap,) + gathered.shape[1:], half)
        for home_z in range(z_num):
            values = jnp.where(mask[:, home_z, None, None], gathered[home_z][None], values)
        return values

    back_half = gathered[:, :chip_rows].reshape(-1, col_num)
    half_rows = back_half.shape[0]
    for_beside = taken(owner ^ 1).reshape(-1, col_num)
    beside = swap_x(
        jnp.concatenate(
            [jnp.where(first, back_half, for_beside[:half_rows]), for_beside[half_rows:]], 0
        )
    )
    chip_results = taken(owner) + beside.reshape(slot_cap, -1, col_num)
    back_half = back_half.reshape(y_num, chip_rows, col_num)
    beside = beside[:half_rows].reshape(back_half.shape)
    back_full = jnp.where(
        even, jnp.stack([back_half, beside], 1), jnp.stack([beside, back_half], 1)
    ).reshape(col_num, col_num)
    chip_update = dot(home[0], back_full, (1, 0)).astype(half)
    chip_results = chip_results.reshape(slot_cap, 3, 2, row_num, col_num)
    for_first = chip_results[:, :, 0].reshape(-1, col_num)
    for_second = jnp.concatenate([chip_update[row_num:], for_first[row_num:]], 0)
    came = swap_cores(jnp.where(first, for_second, for_first))
    update = jnp.where(first, chip_update[:row_num], came[:row_num])
    terms = jnp.where(
        first, came.reshape(slot_cap, 3, row_num, col_num), chip_results[:, :, 1]
    ).astype(jnp.float32)

    new_left = beta_two * left_stat[0] + (1.0 - beta_two) * terms[:, 0]
    new_right = beta_two * right_stat[0] + (1.0 - beta_two) * terms[:, 1]
    new_moment = beta_one * moment[0] + (1.0 - beta_one) * terms[:, 2]
    new_second = beta_two * second[0] + (1.0 - beta_two) * terms[:, 2] * terms[:, 2]
    return (update[None], new_left[None], new_right[None], new_moment[None], new_second[None])


def solution(mesh):
    placed = (
        P("dp", "owner", None, None),
        P(),
        P("owner", None, "dp", None),
        P("owner", None, "dp", None),
        P("owner", None, "dp", None),
        P("owner", None, "dp", None),
        P("owner", None, "dp", None),
        P("owner", None, "dp", None),
    )
    return jax.shard_map(
        on_device,
        mesh=mesh,
        in_specs=placed,
        out_specs=(
            P("owner", "dp", None),
            P("owner", None, "dp", None),
            P("owner", None, "dp", None),
            P("owner", None, "dp", None),
            P("owner", None, "dp", None),
        ),
        check_vma=False,
    )
```

```python
import jax
import jax.numpy as jnp
from jax import lax
from jax.experimental import pallas as pl
from jax.experimental.pallas import tpu as pltpu
from jax.sharding import PartitionSpec as P

beta_one = 0.9
beta_two = 0.95
step_count = 10.0
adam_eps = 1e-08
bias_one = 1.0 - beta_one**step_count
bias_two = 1.0 - beta_two**step_count

LANES = 128
half = jnp.bfloat16


def slot_numbers(assign):
    positions = jnp.arange(assign.shape[0], dtype=jnp.int32)
    matching = assign[:, None] == assign[None, :]
    earlier = positions[None, :] < positions[:, None]
    return jnp.sum((matching & earlier).astype(jnp.int32), axis=1)


def swap_cores(value):
    return lax.ppermute(value, "dp", [(i, i ^ 1) for i in range(lax.axis_size("dp"))])


def place(chip, core, owner):
    return (chip * 2 + core) * lax.axis_size("owner") + owner


def exchange_dp(pieces):
    chips = lax.axis_size("dp") // 2
    groups = [[chip * 2 + core for chip in range(chips)] for core in range(2)]
    return lax.all_to_all(pieces, "dp", 0, 0, axis_index_groups=groups)


def exchange_lines(pieces):
    chips = lax.axis_size("dp") // 2
    owners = lax.axis_size("owner")
    groups = [
        [place(2 * y + x, 0, owner) for y in range(chips // 2)]
        for owner in range(owners)
        for x in range(2)
    ]
    groups += [
        [place(chip, 1, 2 * z + x) for z in range(owners // 2)]
        for chip in range(chips)
        for x in range(2)
    ]
    return lax.all_to_all(pieces, ("dp", "owner"), 0, 0, axis_index_groups=groups)


def swap_x(value):
    chips = lax.axis_size("dp") // 2
    owners = lax.axis_size("owner")
    pairs = []
    for chip in range(chips):
        for owner in range(owners):
            pairs.append((place(chip, 0, owner), place(chip ^ 1, 0, owner)))
            pairs.append((place(chip, 1, owner), place(chip, 1, owner ^ 1)))
    return lax.ppermute(value, ("dp", "owner"), pairs)


def first_payload_kernel(core, grads, left, right, moment, second, slots, payload, wide, sems):
    slot_cap, row_num = left.shape[1:3]
    moves = []
    for slot in range(slot_cap):
        for kind, basis in enumerate((left, right)):
            moves.append(
                pltpu.make_async_copy(
                    basis.at[0, slot], slots.at[slot, kind], sems.at[slot * 2 + kind]
                )
            )
    for kind, state in enumerate((moment, second)):
        moves.append(
            pltpu.make_async_copy(state.at[0], wide.at[kind], sems.at[2 * slot_cap + kind])
        )
    for move in moves:
        move.start()

    @pl.when(core[0] != 0)
    def _():
        move = pltpu.make_async_copy(grads.at[0, 0], payload, sems.at[2 * slot_cap + 2])
        move.start()
        move.wait()

    for move in moves:
        move.wait()
    for slot in range(slot_cap):
        for kind in range(2):
            slots[slot, 2 + kind] = wide[kind, slot].astype(half)

    @pl.when(core[0] == 0)
    def _():
        for slot in range(slot_cap):
            for kind in range(4):
                payload[pl.ds((slot * 4 + kind) * row_num, row_num)] = slots[slot, kind]


def first_payload(core, grads, left, right, moment, second):
    slot_cap, row_num, col_num = left.shape[1:]
    anywhere = pl.BlockSpec(memory_space=pl.ANY)
    vmem = pl.BlockSpec(memory_space=pltpu.VMEM)
    return pl.pallas_call(
        first_payload_kernel,
        out_shape=(
            jax.ShapeDtypeStruct((slot_cap, 4, row_num, col_num), half),
            jax.ShapeDtypeStruct(grads.shape[2:], half),
        ),
        in_specs=[pl.BlockSpec(memory_space=pltpu.SMEM)] + [anywhere] * 5,
        out_specs=(vmem, vmem),
        scratch_shapes=[
            pltpu.VMEM((2, slot_cap, row_num, col_num), jnp.float32),
            pltpu.SemaphoreType.DMA((2 * slot_cap + 3,)),
        ],
        compiler_params=pltpu.CompilerParams(vmem_limit_bytes=60 * 1024 * 1024),
        name="first_payload",
    )(core, grads, left, right, moment, second)


def copies(value, count):
    return jnp.broadcast_to(value[None], (count,) + value.shape)


def dot(left, right, contract):
    return lax.dot_general(
        left, right, ((contract[:1], contract[1:]), ((), ())), preferred_element_type=jnp.float32
    )


def on_device(grad_parts, assign, left_basis, right_basis, left_stat, right_stat, moment, second):
    row_index = lax.axis_index("dp")
    owner = lax.axis_index("owner")
    dp_num = lax.axis_size("dp")
    owner_num = lax.axis_size("owner")
    col_num = grad_parts.shape[3]
    row_num = col_num // dp_num
    slot_cap = left_basis.shape[1]
    chunk_num = col_num // LANES
    chips = dp_num // 2
    chip = row_index // 2
    first = row_index % 2 == 0
    chip_rows = 2 * row_num
    kinds = 4

    grads = grad_parts[0, 0]
    slots, payload = first_payload(
        (row_index % 2).reshape(1), grad_parts, left_basis, right_basis, moment, second
    )
    came = swap_cores(payload)

    y_num = chips // 2
    z_num = owner_num // 2
    pair = (grads.astype(jnp.float32) + came.astype(jnp.float32)).astype(half)
    pair = pair.reshape(y_num, 2, chip_rows, col_num)
    even = chip % 2 == 0
    kept = jnp.where(even, pair[:, 0], pair[:, 1])
    sent = jnp.where(even, pair[:, 1], pair[:, 0]).reshape(-1, col_num)
    slot_rows = slot_cap * kinds * row_num
    chip_slots = jnp.stack([came[:slot_rows].reshape(slots.shape), slots], 2)
    chip_slots = chip_slots.reshape(slot_cap * kinds * chip_rows, col_num)
    sent_num = sent.shape[0]
    payload = jnp.concatenate(
        [jnp.where(first, sent, chip_slots[:sent_num]), chip_slots[sent_num:]], 0
    )
    beside = swap_x(payload)
    numbers = slot_numbers(assign)
    sums = kept.astype(jnp.float32) + beside[:sent_num].reshape(kept.shape).astype(jnp.float32)
    sums = sums.astype(half)

    owner_x = owner % 2
    from_owner = lax.dynamic_index_in_dim(assign.reshape(z_num, 2), owner_x, 1, keepdims=False)
    number = lax.dynamic_index_in_dim(numbers.reshape(z_num, 2), owner_x, 1, keepdims=False)
    code = (number + slot_cap * (from_owner % 2 != owner_x))[:, None, None]
    chip_slots = chip_slots.reshape(slot_cap, kinds * chip_rows, col_num)
    beside = beside.reshape(chip_slots.shape)
    picked = chip_slots[0][None]
    for slot in range(1, slot_cap):
        picked = jnp.where(code == slot, chip_slots[slot][None], picked)
    for slot in range(slot_cap):
        picked = jnp.where(code == slot_cap + slot, beside[slot][None], picked)

    parts = exchange_lines(
        jnp.concatenate(
            [jnp.where(first, sums, picked[:, :chip_rows]), picked[:, chip_rows:]], 1
        )
    )
    grad_rows = jnp.sum(parts[:, :chip_rows].astype(jnp.float32), axis=0).astype(half)
    home = lax.dynamic_index_in_dim(parts, assign[owner] // 2, 0, keepdims=False)

    left_rows, right_rows = home.reshape(kinds, chip_rows, col_num)[:2]
    left_chunks = left_rows.reshape(chip_rows, chunk_num, LANES).transpose(1, 0, 2)
    left_chunks = jnp.broadcast_to(
        left_chunks[:, None], (chunk_num, chips // chunk_num, chip_rows, LANES)
    ).reshape(chips, chip_rows, LANES)
    rows = copies(jnp.where(first, grad_rows, right_rows), chips)
    mine = exchange_dp(jnp.concatenate([rows, left_chunks], 2))
    mine = mine.reshape(col_num, col_num + LANES)
    wide_home = jnp.concatenate([home, home[:, :LANES]], 1)
    other = swap_cores(jnp.concatenate([mine, wide_home], 0))
    home = jnp.where(first, other[col_num:, :col_num], home).reshape(kinds, chip_rows, col_num)
    other = other[:col_num]
    grad_full = jnp.where(first, mine[:, :col_num], other[:, :col_num])
    right_full = jnp.where(first, other[:, :col_num], mine[:, :col_num])
    left_cols = jnp.where(first, other[:, col_num:], mine[:, col_num:])

    chunk = chip // (chips // chunk_num)
    in_chunk = (chip % (chips // chunk_num)) * chip_rows
    own_rows = lambda value: lax.dynamic_slice_in_dim(value, in_chunk, chip_rows, 0)
    turned = own_rows(dot(left_cols, grad_full, (0, 0)).astype(half))
    rotated = dot(turned, right_full, (1, 0))
    home_moment = beta_one * home[2].astype(jnp.float32) + (1.0 - beta_one) * rotated
    home_second = beta_two * home[3].astype(jnp.float32) + (1.0 - beta_two) * rotated * rotated
    direction = (home_moment / bias_one / (jnp.sqrt(home_second / bias_two) + adam_eps)).astype(half)
    back_rows = dot(direction, right_full, (1, 1)).astype(half)
    grad_cols = lax.dynamic_slice_in_dim(grad_full, chunk * LANES, LANES, 1)
    chip_grad_rows = lax.dynamic_slice_in_dim(grad_full, chip * chip_rows, chip_rows, 0)
    left_term = dot(chip_grad_rows, grad_full, (1, 1)).astype(half)
    right_term = own_rows(dot(grad_cols, grad_full, (0, 0)).astype(half))

    results = jnp.concatenate(
        [jnp.where(first, back_rows, left_term), right_term, rotated.astype(half)], 0
    )
    gathered = exchange_lines(copies(results, y_num))

    def taken(target):
        mask = (from_owner == target)[None, :] & (
            number[None, :] == jnp.arange(slot_cap, dtype=jnp.int32)[:, None]
        )
        values = jnp.zeros((slot_cap,) + gathered.shape[1:], half)
        for home_z in range(z_num):
            values = jnp.where(mask[:, home_z, None, None], gathered[home_z][None], values)
        return values

    back_half = gathered[:, :chip_rows].reshape(-1, col_num)
    half_rows = back_half.shape[0]
    for_beside = taken(owner ^ 1).reshape(-1, col_num)
    beside = swap_x(
        jnp.concatenate(
            [jnp.where(first, back_half, for_beside[:half_rows]), for_beside[half_rows:]], 0
        )
    )
    chip_results = taken(owner) + beside.reshape(slot_cap, -1, col_num)
    back_half = back_half.reshape(y_num, chip_rows, col_num)
    beside = beside[:half_rows].reshape(back_half.shape)
    back_full = jnp.where(
        even, jnp.stack([back_half, beside], 1), jnp.stack([beside, back_half], 1)
    ).reshape(col_num, col_num)
    chip_update = dot(home[0], back_full, (1, 0)).astype(half)
    chip_results = chip_results.reshape(slot_cap, 3, 2, row_num, col_num)
    for_first = chip_results[:, :, 0].reshape(-1, col_num)
    for_second = jnp.concatenate([chip_update[row_num:], for_first[row_num:]], 0)
    came = swap_cores(jnp.where(first, for_second, for_first))
    update = jnp.where(first, chip_update[:row_num], came[:row_num])
    terms = jnp.where(
        first, came.reshape(slot_cap, 3, row_num, col_num), chip_results[:, :, 1]
    ).astype(jnp.float32)

    new_left = beta_two * left_stat[0] + (1.0 - beta_two) * terms[:, 0]
    new_right = beta_two * right_stat[0] + (1.0 - beta_two) * terms[:, 1]
    new_moment = beta_one * moment[0] + (1.0 - beta_one) * terms[:, 2]
    new_second = beta_two * second[0] + (1.0 - beta_two) * terms[:, 2] * terms[:, 2]
    return (update[None], new_left[None], new_right[None], new_moment[None], new_second[None])


def solution(mesh):
    placed = (
        P("dp", "owner", None, None),
        P(),
        P("owner", None, "dp", None),
        P("owner", None, "dp", None),
        P("owner", None, "dp", None),
        P("owner", None, "dp", None),
        P("owner", None, "dp", None),
        P("owner", None, "dp", None),
    )
    return jax.shard_map(
        on_device,
        mesh=mesh,
        in_specs=placed,
        out_specs=(
            P("owner", "dp", None),
            P("owner", None, "dp", None),
            P("owner", None, "dp", None),
            P("owner", None, "dp", None),
            P("owner", None, "dp", None),
        ),
        check_vma=False,
    )
```
